32 devices in a mesh: seq: 8 (over z, core), head: 4 (over y, x).
Axes of the slice: x: 2, y: 2, z: 4, core: 2. Of those that a mesh axis runs over, the one named last changes fastest.
Arguments:
- tokens: bfloat16 [512, 3072], P(('seq', 'head')), may hold values from -6 to 6
- w_qkv: bfloat16 [3, 3072, 3072], P(None, 'head'), may hold values from -0.109375 to 0.109375
- lr_weight: bfloat16 [48, 3072], P('head'), may hold values from -0.21875 to 0.21875
- lr_base: float32 [48], P('head'), may hold values from 0.3 to 3
- conv_weight: float32 [2, 4, 3072], P(None, None, 'head'), may hold values from -3 to 3
- w_init: float32 [2, 48, 64, 64], P(None, 'head'), may hold values from -0.75 to 0.75
- w_out: bfloat16 [3072, 3072], P('head'), may hold values from -0.15625 to 0.15625
Outputs:
- mixed: bfloat16 [512, 3072], P(('seq', 'head'))
The draws below stay inside these ranges and needn't reach their ends.
All inputs are finite; a program needn't handle non-finite values.
Results may differ from the reference program's by a relative error of at most 0.018.
Values may be sent and summed in bfloat16 or wider, within the bound.
A program may use at most 128 MiB of HBM per device.

```python
import math
import jax
import jax.numpy as jnp
from jax import lax

D = 3072
HEADS = 48
HD = 64
MB = 16
KERNEL = 4
TOKENS = 512
INNER = 3072
HEAD_DEV = 12
NMB = 32
N_HEAD = 4


def raised(values, own_key, source, target, blocks, factor):
    owner, partner = [(jnp.arange(values.shape[dim]) // (values.shape[dim] // blocks)).reshape([-1 if axis == dim else 1 for axis in range(values.ndim)]) for dim in (source, target)]
    chosen = jax.random.permutation(own_key, blocks)[partner]
    strong = (owner == chosen) | (owner == (partner + blocks // 2) % blocks)
    return jnp.where(strong, factor * values, values)


def block_scale(own_key, dims, split, smallest, largest):
    loudness, own = 1.0, jax.random.fold_in(own_key, 6)
    for dim, shards_of in split:
        steps = jnp.exp(jax.random.uniform(jax.random.fold_in(own, dim), (shards_of,), jnp.float32, smallest / len(split), largest / len(split)))
        loudness = loudness * jnp.repeat(steps, dims[dim] // shards_of).reshape([-1 if axis == dim else 1 for axis in range(len(dims))])
    return loudness


def gaussian(stream_key, extent, width, limit, split=(), kind=jnp.bfloat16):
    values = width * jax.random.normal(stream_key, extent, jnp.float32)
    if split:
        values = values * block_scale(stream_key, extent, split, -0.22, 0.18)
    return jnp.clip(values, -limit, limit).astype(kind)


def bell_draw_with(own_key, shape, width, limit, split, heavy, kind=jnp.bfloat16):
    entries = width * jax.random.normal(own_key, shape, jnp.float32)
    if split:
        entries = entries * block_scale(own_key, shape, split, -0.22, 0.18)
    return jnp.clip(raised(entries, jax.random.fold_in(own_key, 3), *heavy), -limit, limit).astype(kind)


def setup_inputs(seed: int = 0) -> dict:
    streams_of = jax.random.split(jax.random.key(seed), 8)
    tokens = gaussian(streams_of[0], (TOKENS, D), 1.0, 6.0, ((0, 32),))
    w_qkv = gaussian(streams_of[1], (3, INNER, D), D ** -0.5, 0.109375, ((1, 4),))
    lr_weight = gaussian(streams_of[2], (HEADS, D), (D // 4) ** -0.5, 0.21875, ((0, 4),))
    lr_base = jnp.clip(jnp.exp(math.log(3.0) - 2.3025851 * jax.random.uniform(streams_of[3], (HEADS,), jnp.float32) ** block_scale(streams_of[3], (HEADS,), ((0, 4),), -0.2, 0.2)), 0.3, 3.0)
    conv_weight = gaussian(streams_of[4], (2, KERNEL, INNER), 0.5, 3.0, ((2, 4),), jnp.float32)
    w_init = gaussian(streams_of[5], (2, HEADS, HD, HD), HD ** -0.5, 0.75, ((1, 4),), jnp.float32)
    w_out = bell_draw_with(streams_of[6], (INNER, D), INNER ** -0.5, 0.15625, ((0, 4),), (0, 1, 4, 2.0))
    return {"tokens": tokens, "w_qkv": w_qkv, "lr_weight": lr_weight, "lr_base": lr_base, "conv_weight": conv_weight, "w_init": w_init, "w_out": w_out}


PRECISE = lax.Precision.HIGHEST
EPSILON = 1e-05

def compose_maps(earlier_map, later_map):
    return (jnp.matmul(earlier_map[0], later_map[0], precision=PRECISE), jnp.matmul(earlier_map[1], later_map[0], precision=PRECISE) + later_map[1])

def batch_terms(keys_unit, value_rows, step_rates):
    scaled = step_rates[..., None] * keys_unit
    identity_mat = jnp.eye(keys_unit.shape[-1], dtype=jnp.float32)
    transition = identity_mat - jnp.einsum('...thc,...thd->...hcd', scaled, keys_unit, precision=PRECISE)
    offset = jnp.einsum('...thv,...thc->...hvc', value_rows, scaled, precision=PRECISE)
    return (transition, offset)

def batch_output(inner_state, queries, keys_unit, value_rows, step_rates, token_mask):
    applied_q = jnp.einsum('...hvc,...thc->...thv', inner_state, queries, precision=PRECISE)
    applied_k = jnp.einsum('...hvc,...thc->...thv', inner_state, keys_unit, precision=PRECISE)
    errors = applied_k - value_rows
    scores = jnp.einsum('...thc,...shc->...hts', queries, keys_unit, precision=PRECISE)
    scores = scores * token_mask * jnp.swapaxes(step_rates, -1, -2)[..., :, None, :]
    return applied_q - jnp.einsum('...hts,...shv->...thv', scores, errors, precision=PRECISE)

def layer_norm(inputs):
    average = lax.optimization_barrier(jnp.mean(inputs, axis=-1, keepdims=True))
    centred = inputs - average
    variance = lax.optimization_barrier(jnp.mean(centred * centred, axis=-1, keepdims=True))
    return centred / jnp.sqrt(variance + EPSILON)

def causal_conv(raw_rows, taps_row):
    padded = jnp.concatenate([jnp.zeros((KERNEL - 1, raw_rows.shape[1]), jnp.float32), raw_rows.astype(jnp.float32)], axis=0)
    running = jnp.zeros(raw_rows.shape, jnp.float32)
    for position in range(KERNEL):
        running = running + taps_row[position][None, :] * padded[position:position + TOKENS]
    return running

def reference(tokens, w_qkv, lr_weight, lr_base, conv_weight, w_init, w_out):
    projected = [jnp.dot(tokens, jnp.transpose(w_qkv[number]), preferred_element_type=jnp.float32).astype(jnp.bfloat16) for number in range(3)]
    lr_logit = jnp.dot(tokens, jnp.transpose(lr_weight), preferred_element_type=jnp.float32)
    queries = causal_conv(projected[0], conv_weight[0]).reshape(NMB, MB, HEADS, HD)
    keys_conv = causal_conv(projected[1], conv_weight[1]).reshape(TOKENS, HEADS, HD)
    keys_unit = keys_conv / jnp.sqrt((lax.optimization_barrier(jnp.mean(keys_conv * keys_conv, axis=-1, keepdims=True)) + EPSILON) * HD)
    keys_unit = keys_unit.reshape(NMB, MB, HEADS, HD)
    value_rows = projected[2].astype(jnp.float32).reshape(NMB, MB, HEADS, HD)
    step_rates = (lr_base[None, :] * jax.nn.sigmoid(lr_logit) / MB).reshape(NMB, MB, HEADS)
    causal_mask = (jnp.arange(MB)[:, None] >= jnp.arange(MB)[None, :]).astype(jnp.float32)
    anti_mask = jnp.transpose(causal_mask)

    def make_step(token_mask):

        def step_fn(inner_state, minibatch):
            queries_b, keys_b, values_b, rates_b = minibatch
            result = batch_output(inner_state, queries_b, keys_b, values_b, rates_b, token_mask)
            transition, offset = batch_terms(keys_b, values_b, rates_b)
            return (jnp.matmul(inner_state, transition, precision=PRECISE) + offset, result)
        return step_fn
    inputs_all = (queries, keys_unit, value_rows, step_rates)
    unused_f, fwd_out = lax.scan(make_step(causal_mask), w_init[0], inputs_all)
    unused_r, rev_out = lax.scan(make_step(anti_mask), w_init[1], inputs_all, reverse=True)
    hidden = (layer_norm(fwd_out) + layer_norm(rev_out)).reshape(TOKENS, INNER).astype(jnp.bfloat16)
    grouped = jnp.transpose(hidden.reshape(TOKENS, N_HEAD, HEAD_DEV * HD), (1, 0, 2))
    weights = w_out.reshape(N_HEAD, HEAD_DEV * HD, D)

    def add_group(running, group_pair):
        rounded = jnp.dot(group_pair[0], group_pair[1], preferred_element_type=jnp.float32).astype(jnp.bfloat16)
        rounded = lax.optimization_barrier(rounded)
        return (running + rounded.astype(jnp.float32), None)
    summed, unused_g = lax.scan(add_group, jnp.zeros((TOKENS, D), jnp.float32), (grouped, weights))
    return summed.astype(jnp.bfloat16)
```

```python
import functools

import jax
import jax.numpy as jnp
from jax import lax
from jax.experimental import pallas as pl
from jax.experimental.pallas import tpu as pltpu
from jax.sharding import PartitionSpec as P

MB = 16
KERNEL = 4
EPSILON = 1e-05
LANES = 128
MESH = pl.DeviceIdType.MESH
F32, BF16 = jnp.float32, jnp.bfloat16


def mm(a, b):
    return jnp.dot(a, b, preferred_element_type=F32)


def layer(cfg, tok, wqkv, lrw, lrb, cw, winit, wout, out,
          xbuf, halo, xs, xt, wv, wov, lrwv, lrbv, cwv, wi, srate,
          maps, adds, wrecv, wsend, ht, pbuf, rbuf,
          lsem, wsem, tsend, trecv, hsend, hrecv, rsend, rrecv, psend, precv):
    n, nh, heads, hd, group, chunks = cfg
    own, depth = tok.shape
    rows = own * nh
    inner = heads * hd
    groups = heads // group
    g, me = lax.axis_index("seq"), lax.axis_index("head")
    not_first, not_last = g > 0, g < n - 1
    last_head = me == nh - 1

    small = [pltpu.make_async_copy(a, b, lsem.at[k]) for k, (a, b) in enumerate((
        (tok, xbuf.at[me]), (lrw, lrwv), (lrb, lrbv), (cw, cwv), (winit, wi)))]
    for copy in small:
        copy.start()
    weights = []
    for gi in range(groups):
        span = pl.ds(gi * group * hd, group * hd)
        weights.append([pltpu.make_async_copy(wqkv.at[c, span], wv.at[c, span], wsem.at[gi, c])
                        for c in range(3)])
        for copy in weights[-1]:
            copy.start()
    out_weight = pltpu.make_async_copy(wout, wov, lsem.at[5])
    out_weight.start()

    barrier = pltpu.get_barrier_semaphore()
    for i in range(1, nh):
        pl.semaphore_signal(barrier, inc=1, device_id=(g, lax.rem(me + i, nh)), device_id_type=MESH)

    @pl.when(not_first)
    def _():
        pl.semaphore_signal(barrier, inc=1, device_id=(g - 1, me), device_id_type=MESH)
        pl.semaphore_signal(barrier, inc=1, device_id=(g - 1, nh - 1), device_id_type=MESH)

    @pl.when(not_last)
    def _():
        pl.semaphore_signal(barrier, inc=1, device_id=(g + 1, me), device_id_type=MESH)

    pl.semaphore_wait(barrier, (nh - 1) + jnp.where(not_first, 1, 0) + jnp.where(not_last, 1, 0)
                      + jnp.where(last_head & not_last, nh, 0))

    def token_copy(i, slot):
        return pltpu.make_async_remote_copy(
            src_ref=tok, dst_ref=xbuf.at[slot], send_sem=tsend.at[i], recv_sem=trecv.at[i],
            device_id=(g, lax.rem(me + i, nh)), device_id_type=MESH)

    def halo_copy(h):
        return pltpu.make_async_remote_copy(
            src_ref=tok, dst_ref=halo, send_sem=hsend.at[h], recv_sem=hrecv.at[0],
            device_id=(g + 1, h), device_id_type=MESH)

    for i in range(1, nh):
        token_copy(i, me).start()

    @pl.when(last_head & not_last)
    def _():
        for h in range(nh):
            halo_copy(h).start()

    @pl.when(jnp.logical_not(not_first))
    def _():
        halo[...] = jnp.zeros_like(halo)

    xs[pl.ds(rows, LANES - own - rows), :] = jnp.zeros((LANES - own - rows, depth), F32)
    for copy in small:
        copy.wait()
    for i in range(1, nh):
        token_copy(i, lax.rem(me + nh - i, nh)).wait_recv()

    @pl.when(not_first)
    def _():
        halo_copy(0).wait_recv()

    for p in range(nh):
        xs[pl.ds(p * own, own), :] = xbuf[p].astype(F32)
    xs[pl.ds(LANES - own, own), :] = halo[...].astype(F32)
    for j in range(depth // LANES):
        cols = pl.ds(j * LANES, LANES)
        xt[cols, :] = xs[:, cols].T.astype(BF16)

    logit = mm(lrwv[...], xt[...])
    srate[...] = jnp.sqrt(lrbv[...] * jax.nn.sigmoid(logit) / MB)

    at_s = lax.broadcasted_iota(jnp.int32, (rows, rows), 0)
    at_t = lax.broadcasted_iota(jnp.int32, (rows, rows), 1)
    earlier = (at_s // MB) < (at_t // MB)
    causal, anti = at_s <= at_t, at_s >= at_t
    eye = (at_s == at_t).astype(F32)

    def convolved(gi, c):
        weights[gi][c].wait()
        span = pl.ds(gi * group * hd, group * hd)
        rounded = mm(wv[c, span, :], xt[...]).astype(BF16).astype(F32)
        if c == 2:
            return rounded
        taps = cwv[span, :]
        total = taps[:, c * KERNEL + KERNEL - 1:c * KERNEL + KERNEL] * rounded
        for p in range(KERNEL - 1):
            at = c * KERNEL + p
            total = total + taps[:, at:at + 1] * pltpu.roll(rounded, KERNEL - 1 - p, 1)
        return total

    for gi in range(groups):
        q_all, k_all, v_all = [convolved(gi, c) for c in range(3)]
        each = range(group)
        part = [slice(j * hd, (j + 1) * hd) for j in each]
        q = [q_all[s, :rows] for s in part]
        k = [k_all[s, :rows] for s in part]
        root = [srate[pl.ds(gi * group + j, 1), :][:, :rows] for j in each]
        k = [k[j] * (root[j] * lax.rsqrt(jnp.sum(k[j] * k[j], axis=0, keepdims=True)
                                         + EPSILON * hd)) for j in each]
        v = [(v_all[part[j], :rows] * root[j]).astype(BF16) for j in each]
        kt = [a.T.astype(BF16) for a in k]
        kb = [a.astype(BF16) for a in k]
        qb = [a.astype(BF16) for a in q]
        gram = [mm(kt[j], jnp.concatenate([kb[j], qb[j]], axis=1)) for j in each]
        one = [jnp.where(earlier, a[:, :rows], 0.0) for a in gram]
        oneb = [a.astype(BF16) for a in one]
        two = [mm(a, a) for a in oneb]
        three = [mm(oneb[j], two[j].astype(BF16)) for j in each]
        inv = [eye - one[j] + two[j] - three[j] for j in each]
        both = [jnp.concatenate([a, a.T], axis=1).astype(BF16) for a in inv]
        kv = [mm(jnp.concatenate([kb[j], v[j]], axis=0), both[j]) for j in each]
        for way, mask in ((0, causal), (1, anti)):
            left = [a[:, way * rows:(way + 1) * rows].astype(BF16) for a in kv]
            right = [jnp.concatenate(
                [kt[j], jnp.where(mask, gram[j][:, rows:], 0.0).astype(BF16)], axis=1) for j in each]
            made = [mm(left[j], right[j]) for j in each]
            for j in each:
                head = gi * group + j
                base = jnp.concatenate([jnp.zeros((hd, hd), F32), q[j]], axis=1)
                maps[way, head] = (base - made[j][:hd]).astype(BF16)
                adds[way, head] = made[j][hd:]

    def packed(a):
        return jnp.concatenate([a[:hd // 2], a[hd // 2:]], axis=1)

    def unpacked(a):
        return jnp.concatenate([a[:, :hd], a[:, hd:]], axis=0)

    @pl.when(jnp.logical_not(not_first))
    def _():
        for h in range(heads):
            wrecv[0, h] = packed(wi[0, h])

    @pl.when(jnp.logical_not(not_last))
    def _():
        for h in range(heads):
            wrecv[1, h] = packed(wi[1, h])

    def state_copy(way, gi):
        span = pl.ds(gi * group, group)
        return pltpu.make_async_remote_copy(
            src_ref=wsend.at[way, span], dst_ref=wrecv.at[way, span],
            send_sem=rsend.at[way, gi], recv_sem=rrecv.at[way, gi],
            device_id=(g + 1 - 2 * way, me), device_id_type=MESH)

    ways = []
    for d in range(2):
        way = jnp.where(g < n // 2, d, 1 - d)
        starts = jnp.where(way == 0, g, n - 1 - g) == 0
        ends = jnp.where(way == 0, n - 1 - g, g) == 0
        ways.append((way, ends))
        for gi in range(groups):
            @pl.when(jnp.logical_not(starts))
            def _():
                state_copy(way, gi).wait_recv()

            reach = []
            for j in range(group):
                head = gi * group + j
                state = unpacked(wrecv[way, head])
                new = mm(state.astype(BF16), maps[way, head]) + adds[way, head]
                wsend[way, head] = packed(state + new[:, :hd])
                reach.append(new[:, hd:])

            @pl.when(jnp.logical_not(ends))
            def _():
                state_copy(way, gi).start()

            for j in range(group):
                at = pl.ds((gi * group + j) * hd, hd)
                centred = reach[j] - jnp.mean(reach[j], axis=0, keepdims=True)
                spread = jnp.mean(centred * centred, axis=0, keepdims=True)
                normed = centred * lax.rsqrt(spread + EPSILON)
                if d == 0:
                    ht[at, pl.ds(0, rows)] = normed
                else:
                    ht[at, pl.ds(0, rows)] = ht[at, pl.ds(0, rows)] + normed

    hidden = jnp.concatenate(
        [ht[pl.ds(j * LANES, LANES), :].T[:rows] for j in range(ht.shape[0] // LANES)], axis=1)
    hidden = hidden[:, :inner].astype(BF16)
    out_weight.wait()

    def share_copy(j, i, to, slot):
        cols = pl.ds(j * (depth // chunks), depth // chunks)
        return pltpu.make_async_remote_copy(
            src_ref=pbuf.at[to, :, cols], dst_ref=rbuf.at[slot, :, cols],
            send_sem=psend.at[j, i], recv_sem=precv.at[j, i],
            device_id=(g, to), device_id_type=MESH)

    for j in range(chunks):
        cols = pl.ds(j * (depth // chunks), depth // chunks)
        share = mm(hidden, wov[:, cols])
        for p in range(nh):
            pbuf[p, :, cols] = share[p * own:(p + 1) * own].astype(BF16)
        for i in range(1, nh):
            share_copy(j, i, lax.rem(me + i, nh), me).start()

    for j in range(chunks):
        cols = pl.ds(j * (depth // chunks), depth // chunks)
        total = pbuf[me, :, cols].astype(F32)
        for i in range(1, nh):
            sender = lax.rem(me + nh - i, nh)
            share_copy(j, i, lax.rem(me + i, nh), sender).wait_recv()
            total = total + rbuf[sender, :, cols].astype(F32)
        out[:, cols] = total.astype(BF16)

    for i in range(1, nh):
        token_copy(i, me).wait_send()
        for j in range(chunks):
            share_copy(j, i, lax.rem(me + i, nh), me).wait_send()

    @pl.when(last_head & not_last)
    def _():
        for h in range(nh):
            halo_copy(h).wait_send()

    for way, ends in ways:
        @pl.when(jnp.logical_not(ends))
        def _():
            for gi in range(groups):
                state_copy(way, gi).wait_send()


def shards(n, nh, tokens, w_qkv, lr_weight, lr_base, conv_weight, w_init, w_out):
    own, depth = tokens.shape
    heads, hd = w_init.shape[1], w_init.shape[2]
    inner = heads * hd
    rows = own * nh
    group = max(k for k in (1, 2, 3, 4) if heads % k == 0)
    groups = heads // group
    chunks = 2
    padded = -(-inner // LANES) * LANES
    taps = jnp.transpose(conv_weight.reshape(2 * KERNEL, inner))
    any_space = pl.BlockSpec(memory_space=pl.ANY)
    dma = pltpu.SemaphoreType.DMA
    return pl.pallas_call(
        functools.partial(layer, (n, nh, heads, hd, group, chunks)),
        out_shape=jax.ShapeDtypeStruct((own, depth), BF16),
        in_specs=[any_space] * 7,
        out_specs=pl.BlockSpec(memory_space=pltpu.VMEM),
        scratch_shapes=[
            pltpu.VMEM((nh, own, depth), BF16),
            pltpu.VMEM((own, depth), BF16),
            pltpu.VMEM((LANES, depth), F32),
            pltpu.VMEM((depth, LANES), BF16),
            pltpu.VMEM(w_qkv.shape, BF16),
            pltpu.VMEM(w_out.shape, BF16),
            pltpu.VMEM(lr_weight.shape, BF16),
            pltpu.VMEM((heads, 1), F32),
            pltpu.VMEM((inner, 2 * KERNEL), F32),
            pltpu.VMEM(w_init.shape, F32),
            pltpu.VMEM((heads, LANES), F32),
            pltpu.VMEM((2, heads, hd, hd + rows), BF16),
            pltpu.VMEM((2, heads, hd, hd + rows), F32),
            pltpu.VMEM((2, heads, hd // 2, 2 * hd), F32),
            pltpu.VMEM((2, heads, hd // 2, 2 * hd), F32),
            pltpu.VMEM((padded, LANES), F32),
            pltpu.VMEM((nh, own, depth), BF16),
            pltpu.VMEM((nh, own, depth), BF16),
            dma((6,)),
            dma((groups, 3)),
            dma((nh,)),
            dma((nh,)),
            dma((nh,)),
            dma((1,)),
            dma((2, groups)),
            dma((2, groups)),
            dma((chunks, nh)),
            dma((chunks, nh)),
        ],
        compiler_params=pltpu.CompilerParams(
            collective_id=0, has_side_effects=True, vmem_limit_bytes=52 * 2 ** 20),
    )(tokens, w_qkv, lr_weight, lr_base.reshape(heads, 1), taps, w_init, w_out)


def solution(mesh):
    placed = (
        P(("seq", "head"), None),
        P(None, "head", None),
        P("head", None),
        P("head"),
        P(None, None, "head"),
        P(None, "head", None, None),
        P("head", None),
    )
    return jax.shard_map(
        functools.partial(shards, mesh.shape["seq"], mesh.shape["head"]),
        mesh=mesh, in_specs=placed, out_specs=P(("seq", "head"), None), check_vma=False
    )
```

```python
import functools

import jax
import jax.numpy as jnp
from jax import lax
from jax.experimental import pallas as pl
from jax.experimental.pallas import tpu as pltpu
from jax.sharding import PartitionSpec as P

MB = 16
KERNEL = 4
EPSILON = 1e-05
LANES = 128
MESH = pl.DeviceIdType.MESH
F32, BF16 = jnp.float32, jnp.bfloat16


def mm(a, b):
    return jnp.dot(a, b, preferred_element_type=F32)


def layer(cfg, tok, wqkv, lrw, lrb, cw, winit, wout, out,
          xbuf, halo, xs, xt, wv, wov, lrwv, cwv, cwt, taps_ref, wi, gate,
          maps, adds, states, sending, reach, kept, pbuf, rbuf,
          lsem, wsem, tsend, trecv, hsend, hrecv, rsend, rrecv, psend, precv):
    n, nh, heads, hd, pair_group, chunks = cfg
    own, depth = tok.shape
    rows = own * nh
    inner = heads * hd
    pairs = (heads + 1) // 2
    groups = pairs // pair_group
    wide = 2 * hd
    g, me = lax.axis_index("seq"), lax.axis_index("head")
    not_first, not_last = g > 0, g < n - 1
    last_head = me == nh - 1

    small = [pltpu.make_async_copy(a, b, lsem.at[k]) for k, (a, b) in enumerate((
        (tok, xbuf.at[me]), (lrw, lrwv), (cw, cwv), (winit, wi)))]
    for copy in small:
        copy.start()
    weights = []
    for gi in range(groups):
        start = gi * pair_group * wide
        span = pl.ds(start, min(pair_group * wide, inner - start))
        weights.append([pltpu.make_async_copy(wqkv.at[c, span], wv.at[c, span], wsem.at[gi, c])
                        for c in range(3)])
        for copy in weights[-1]:
            copy.start()
    out_weight = pltpu.make_async_copy(wout, wov, lsem.at[4])
    out_weight.start()

    barrier = pltpu.get_barrier_semaphore()
    for i in range(1, nh):
        pl.semaphore_signal(barrier, inc=1, device_id=(g, lax.rem(me + i, nh)), device_id_type=MESH)

    @pl.when(not_first)
    def _():
        pl.semaphore_signal(barrier, inc=1, device_id=(g - 1, me), device_id_type=MESH)
        pl.semaphore_signal(barrier, inc=1, device_id=(g - 1, nh - 1), device_id_type=MESH)

    @pl.when(not_last)
    def _():
        pl.semaphore_signal(barrier, inc=1, device_id=(g + 1, me), device_id_type=MESH)

    pl.semaphore_wait(barrier, (nh - 1) + jnp.where(not_first, 1, 0) + jnp.where(not_last, 1, 0)
                      + jnp.where(last_head & not_last, nh, 0))

    def token_copy(i, slot):
        return pltpu.make_async_remote_copy(
            src_ref=tok, dst_ref=xbuf.at[slot], send_sem=tsend.at[i], recv_sem=trecv.at[i],
            device_id=(g, lax.rem(me + i, nh)), device_id_type=MESH)

    def halo_copy(h):
        return pltpu.make_async_remote_copy(
            src_ref=tok, dst_ref=halo, send_sem=hsend.at[h], recv_sem=hrecv.at[0],
            device_id=(g + 1, h), device_id_type=MESH)

    for i in range(1, nh):
        token_copy(i, me).start()

    @pl.when(last_head & not_last)
    def _():
        for h in range(nh):
            halo_copy(h).start()

    @pl.when(jnp.logical_not(not_first))
    def _():
        halo[...] = jnp.zeros_like(halo)

    xs[pl.ds(rows, LANES - own - rows), :] = jnp.zeros((LANES - own - rows, depth), F32)
    for copy in small:
        copy.wait()

    cwt[...] = jnp.zeros_like(cwt)
    for c in range(2):
        cwt[pl.ds(c * KERNEL, KERNEL), pl.ds(0, inner)] = cwv[c]
    for j in range(pairs):
        taps_ref[pl.ds(j * LANES, LANES), :] = cwt[:, pl.ds(j * LANES, LANES)].T

    for way, outer in ((0, jnp.logical_not(not_first)), (1, jnp.logical_not(not_last))):
        @pl.when(outer)
        def _():
            for p in range(pairs):
                second = wi[way, 2 * p + 1] if 2 * p + 1 < heads else jnp.zeros((hd, hd), F32)
                states[way, p] = jnp.concatenate([wi[way, 2 * p], second], axis=1).astype(BF16)

    for i in range(1, nh):
        token_copy(i, lax.rem(me + nh - i, nh)).wait_recv()

    @pl.when(not_first)
    def _():
        halo_copy(0).wait_recv()

    for p in range(nh):
        xs[pl.ds(p * own, own), :] = xbuf[p].astype(F32)
    xs[pl.ds(LANES - own, own), :] = halo[...].astype(F32)
    for j in range(depth // LANES):
        cols = pl.ds(j * LANES, LANES)
        xt[cols, :] = xs[:, cols].T.astype(BF16)

    gate[...] = jax.nn.sigmoid(mm(lrwv[...], xt[...]))

    at_s = lax.broadcasted_iota(jnp.int32, (wide, wide), 0)
    at_t = lax.broadcasted_iota(jnp.int32, (wide, wide), 1)
    upper, left_half = at_s < hd, at_t < rows
    same = upper == left_half
    earlier = same & ((at_s // MB) < (at_t // MB))
    causal, anti = same & (at_s <= at_t), same & (at_s >= at_t)
    eye = (at_s == at_t).astype(F32)
    row_left = left_half[:1]

    def diagonal(a):
        return jnp.where(same, jnp.where(upper, a, pltpu.roll(a, rows, 1)), 0.0)

    def root_rate(p):
        first = gate[pl.ds(2 * p, 1), :] * lrb[2 * p]
        if 2 * p + 1 == heads:
            return jnp.sqrt(jnp.where(row_left, first, 0.0) / MB)
        second = gate[pl.ds(2 * p + 1, 1), :] * lrb[2 * p + 1]
        return jnp.sqrt(jnp.where(row_left, first, pltpu.roll(second, rows, 1)) / MB)

    def convolved(gi, c):
        weights[gi][c].wait()
        span = pl.ds(gi * pair_group * wide, pair_group * wide)
        rounded = mm(wv[c, span, :], xt[...]).astype(BF16).astype(F32)
        if inner < pairs * wide:
            row = lax.broadcasted_iota(jnp.int32, rounded.shape, 0) + gi * pair_group * wide
            rounded = jnp.where(row < inner, rounded, 0.0)
        if c == 2:
            return rounded
        taps = taps_ref[span, :]
        total = taps[:, c * KERNEL + KERNEL - 1:c * KERNEL + KERNEL] * rounded
        for p in range(KERNEL - 1):
            at = c * KERNEL + p
            total = total + taps[:, at:at + 1] * pltpu.roll(rounded, KERNEL - 1 - p, 1)
        return total

    for gi in range(groups):
        q_all, k_all, v_all = [convolved(gi, c) for c in range(3)]
        each = range(pair_group)
        part = [slice(j * wide, (j + 1) * wide) for j in each]
        root = [root_rate(gi * pair_group + j) for j in each]
        q = [diagonal(q_all[s]) for s in part]
        k = [diagonal(k_all[s]) for s in part]
        k = [k[j] * (root[j] * lax.rsqrt(jnp.sum(k[j] * k[j], axis=0, keepdims=True)
                                         + EPSILON * hd)) for j in each]
        v = [(diagonal(v_all[part[j]]) * root[j]).astype(BF16) for j in each]
        kt = [a.T.astype(BF16) for a in k]
        kb = [a.astype(BF16) for a in k]
        qb = [a.astype(BF16) for a in q]
        gram = [mm(kt[j], jnp.concatenate([kb[j], qb[j]], axis=1)) for j in each]
        one = [jnp.where(earlier, a[:, :wide], 0.0) for a in gram]
        oneb = [a.astype(BF16) for a in one]
        two = [mm(a, a) for a in oneb]
        three = [mm(oneb[j], two[j].astype(BF16)) for j in each]
        inv = [eye - one[j] + two[j] - three[j] for j in each]
        both = [jnp.concatenate([a, a.T], axis=1).astype(BF16) for a in inv]
        kv = [mm(jnp.concatenate([kb[j], v[j]], axis=0), both[j]) for j in each]
        for way, mask in ((0, causal), (1, anti)):
            lhs = [a[:, way * wide:(way + 1) * wide].astype(BF16) for a in kv]
            rhs = [jnp.concatenate(
                [kt[j], jnp.where(mask, gram[j][:, wide:], 0.0).astype(BF16)], axis=1) for j in each]
            made = [mm(lhs[j], rhs[j]) for j in each]
            for j in each:
                p = gi * pair_group + j
                maps[way, p, :, pl.ds(0, wide)] = (-made[j][:wide, :wide]).astype(BF16)
                maps[way, p, :, pl.ds(wide, wide)] = (q[j] - made[j][:wide, wide:]).astype(BF16)
                adds[way, p] = made[j][wide:wide + hd] + made[j][wide + hd:]

    def state_copy(way, gi):
        span = pl.ds(gi * pair_group, pair_group)
        return pltpu.make_async_remote_copy(
            src_ref=sending.at[way, span], dst_ref=states.at[way, span],
            send_sem=rsend.at[way, gi], recv_sem=rrecv.at[way, gi],
            device_id=(g + 1 - 2 * way, me), device_id_type=MESH)

    ways, normed = [], []
    for d in range(2):
        way = jnp.where(g < n // 2, d, 1 - d)
        starts = jnp.where(way == 0, g, n - 1 - g) == 0
        ends = jnp.where(way == 0, n - 1 - g, g) == 0
        ways.append((way, ends))
        for gi in range(groups):
            @pl.when(jnp.logical_not(starts))
            def _():
                state_copy(way, gi).wait_recv()

            mine = range(gi * pair_group, (gi + 1) * pair_group)
            old = [states[way, p] for p in mine]
            new = [mm(a, maps[way, p]) + adds[way, p] for a, p in zip(old, mine)]
            for a, b, p in zip(old, new, mine):
                sending[way, p] = (a.astype(F32) + b[:, :wide]).astype(BF16)

            @pl.when(jnp.logical_not(ends))
            def _():
                state_copy(way, gi).start()

            for b, p in zip(new, mine):
                reach[p] = b[:, wide:]

        for p in range(pairs):
            got = reach[p]
            centred = got - jnp.mean(got, axis=0, keepdims=True)
            spread = jnp.mean(centred * centred, axis=0, keepdims=True)
            scaled = centred * lax.rsqrt(spread + EPSILON)
            if d == 0:
                kept[p] = scaled
            else:
                normed.append(scaled + kept[p])

    turned = [a.T for a in normed]
    hidden = jnp.concatenate(
        [jnp.concatenate([a[:rows], a[rows:]], axis=1) for a in turned], axis=1)
    hidden = hidden[:, :inner].astype(BF16)
    out_weight.wait()

    def share_copy(j, i, to, slot):
        cols = pl.ds(j * (depth // chunks), depth // chunks)
        return pltpu.make_async_remote_copy(
            src_ref=pbuf.at[to, :, cols], dst_ref=rbuf.at[slot, :, cols],
            send_sem=psend.at[j, i], recv_sem=precv.at[j, i],
            device_id=(g, to), device_id_type=MESH)

    for j in range(chunks):
        cols = pl.ds(j * (depth // chunks), depth // chunks)
        share = mm(hidden, wov[:, cols])
        for p in range(nh):
            pbuf[p, :, cols] = share[p * own:(p + 1) * own].astype(BF16)
        for i in range(1, nh):
            share_copy(j, i, lax.rem(me + i, nh), me).start()

    for j in range(chunks):
        cols = pl.ds(j * (depth // chunks), depth // chunks)
        total = pbuf[me, :, cols].astype(F32)
        for i in range(1, nh):
            sender = lax.rem(me + nh - i, nh)
            share_copy(j, i, lax.rem(me + i, nh), sender).wait_recv()
            total = total + rbuf[sender, :, cols].astype(F32)
        out[:, cols] = total.astype(BF16)

    for i in range(1, nh):
        token_copy(i, me).wait_send()
        for j in range(chunks):
            share_copy(j, i, lax.rem(me + i, nh), me).wait_send()

    @pl.when(last_head & not_last)
    def _():
        for h in range(nh):
            halo_copy(h).wait_send()

    for way, ends in ways:
        @pl.when(jnp.logical_not(ends))
        def _():
            for gi in range(groups):
                state_copy(way, gi).wait_send()


def shards(n, nh, tokens, w_qkv, lr_weight, lr_base, conv_weight, w_init, w_out):
    own, depth = tokens.shape
    heads, hd = w_init.shape[1], w_init.shape[2]
    inner = heads * hd
    pairs = (heads + 1) // 2
    padded = pairs * 2 * hd
    pair_group = 2 if pairs % 2 == 0 else 1
    groups = pairs // pair_group
    chunks = 2
    wide = 2 * hd
    hbm = pl.BlockSpec(memory_space=pltpu.HBM)
    smem = pl.BlockSpec(memory_space=pltpu.SMEM)
    dma = pltpu.SemaphoreType.DMA
    return pl.pallas_call(
        functools.partial(layer, (n, nh, heads, hd, pair_group, chunks)),
        out_shape=jax.ShapeDtypeStruct((own, depth), BF16),
        in_specs=[hbm, hbm, hbm, smem, hbm, hbm, hbm],
        out_specs=pl.BlockSpec(memory_space=pltpu.VMEM),
        scratch_shapes=[
            pltpu.VMEM((nh, own, depth), BF16),
            pltpu.VMEM((own, depth), BF16),
            pltpu.VMEM((LANES, depth), F32),
            pltpu.VMEM((depth, LANES), BF16),
            pltpu.VMEM((3, padded, depth), BF16),
            pltpu.VMEM(w_out.shape, BF16),
            pltpu.VMEM(lr_weight.shape, BF16),
            pltpu.VMEM(conv_weight.shape, F32),
            pltpu.VMEM((LANES, padded), F32),
            pltpu.VMEM((padded, LANES), F32),
            pltpu.VMEM(w_init.shape, F32),
            pltpu.VMEM((heads, LANES), F32),
            pltpu.VMEM((2, pairs, wide, 2 * wide), BF16),
            pltpu.VMEM((2, pairs, hd, 2 * wide), F32),
            pltpu.VMEM((2, pairs, hd, wide), BF16),
            pltpu.VMEM((2, pairs, hd, wide), BF16),
            pltpu.VMEM((pairs, hd, wide), F32),
            pltpu.VMEM((pairs, hd, wide), F32),
            pltpu.VMEM((nh, own, depth), BF16),
            pltpu.VMEM((nh, own, depth), BF16),
            dma((5,)),
            dma((groups, 3)),
            dma((nh,)),
            dma((nh,)),
            dma((nh,)),
            dma((1,)),
            dma((2, groups)),
            dma((2, groups)),
            dma((chunks, nh)),
            dma((chunks, nh)),
        ],
        compiler_params=pltpu.CompilerParams(
            collective_id=0, has_side_effects=True, vmem_limit_bytes=60 * 2 ** 20),
    )(tokens, w_qkv, lr_weight, lr_base, conv_weight, w_init, w_out)


def solution(mesh):
    placed = (
        P(("seq", "head"), None),
        P(None, "head", None),
        P("head", None),
        P("head"),
        P(None, None, "head"),
        P(None, "head", None, None),
        P("head", None),
    )
    return jax.shard_map(
        functools.partial(shards, mesh.shape["seq"], mesh.shape["head"]),
        mesh=mesh, in_specs=placed, out_specs=P(("seq", "head"), None), check_vma=False
    )
```

```python
import functools

import jax
import jax.numpy as jnp
from jax import lax
from jax.experimental import pallas as pl
from jax.experimental.pallas import tpu as pltpu
from jax.sharding import PartitionSpec as P

MB = 16
KERNEL = 4
EPSILON = 1e-05
LANES = 128
MESH = pl.DeviceIdType.MESH
F32, BF16 = jnp.float32, jnp.bfloat16


def mm(a, b):
    return jnp.dot(a, b, preferred_element_type=F32)


def mm_rows(a, b):
    return lax.dot_general(a, b, (((1,), (1,)), ((), ())), preferred_element_type=F32)


def layer(cfg, tok, wqkv, lrw, lrb, cw, winit, wout, out,
          xbuf, rim, halo, xs, xt, wv, wov, lrwv, cwv, cwt, taps_ref, wi, gate,
          maps, adds, states, sending, reach, kept, pbuf, rbuf,
          lsem, wsem, tsend, trecv, hsend, hrecv, rsend, rrecv, psend, precv):
    n, nh, heads, hd, pair_group, chunks = cfg
    own, depth = tok.shape
    rows = own * nh
    inner = heads * hd
    pairs = (heads + 1) // 2
    groups = pairs // pair_group
    wide = 2 * hd
    g, me = lax.axis_index("seq"), lax.axis_index("head")
    not_first, not_last = g > 0, g < n - 1
    last_head = me == nh - 1

    small = [pltpu.make_async_copy(a, b, lsem.at[k]) for k, (a, b) in enumerate((
        (tok, xbuf.at[me]), (lrw, lrwv), (cw, cwv), (winit, wi)))]
    for copy in small:
        copy.start()
    weights = []
    for c in range(3):
        weights.append(pltpu.make_async_copy(wqkv.at[c], wv.at[c, pl.ds(0, inner)], wsem.at[c]))
        weights[c].start()
    out_weight = pltpu.make_async_copy(wout, wov, lsem.at[4])
    out_weight.start()

    barrier = pltpu.get_barrier_semaphore()
    for i in range(1, nh):
        pl.semaphore_signal(barrier, inc=1, device_id=(g, lax.rem(me + i, nh)), device_id_type=MESH)

    @pl.when(not_first)
    def _():
        pl.semaphore_signal(barrier, inc=1, device_id=(g - 1, me), device_id_type=MESH)
        pl.semaphore_signal(barrier, inc=1, device_id=(g - 1, nh - 1), device_id_type=MESH)

    @pl.when(not_last)
    def _():
        pl.semaphore_signal(barrier, inc=1, device_id=(g + 1, me), device_id_type=MESH)

    pl.semaphore_wait(barrier, (nh - 1) + jnp.where(not_first, 1, 0) + jnp.where(not_last, 1, 0)
                      + jnp.where(last_head & not_last, nh, 0))

    def token_copy(i, slot):
        return pltpu.make_async_remote_copy(
            src_ref=tok, dst_ref=xbuf.at[slot], send_sem=tsend.at[i], recv_sem=trecv.at[i],
            device_id=(g, lax.rem(me + i, nh)), device_id_type=MESH)

    def halo_copy(h):
        return pltpu.make_async_remote_copy(
            src_ref=rim, dst_ref=halo, send_sem=hsend.at[h], recv_sem=hrecv.at[0],
            device_id=(g + 1, h), device_id_type=MESH)

    for i in range(1, nh):
        token_copy(i, me).start()

    small[0].wait()
    rim_rows = KERNEL - 1
    piece = depth // rim_rows
    mine_last = xbuf[me].astype(F32)[own - rim_rows:]
    rim[...] = jnp.concatenate(
        [mine_last[r:r + 1, c * piece:(c + 1) * piece] for r in range(rim_rows) for c in range(rim_rows)]
        + [jnp.zeros((rim.shape[0] - rim_rows * rim_rows, piece), F32)], axis=0).astype(BF16)

    @pl.when(last_head & not_last)
    def _():
        for h in range(nh):
            halo_copy(h).start()

    @pl.when(jnp.logical_not(not_first))
    def _():
        halo[...] = jnp.zeros_like(halo)

    for copy in small[1:]:
        copy.wait()

    cwt[...] = jnp.zeros_like(cwt)
    for c in range(2):
        cwt[pl.ds(c * KERNEL, KERNEL), pl.ds(0, inner)] = cwv[c]
    for j in range(pairs):
        taps_ref[pl.ds(j * LANES, LANES), :] = cwt[:, pl.ds(j * LANES, LANES)].T

    for way, outer in ((0, jnp.logical_not(not_first)), (1, jnp.logical_not(not_last))):
        @pl.when(outer)
        def _():
            for p in range(pairs):
                second = wi[way, 2 * p + 1] if 2 * p + 1 < heads else jnp.zeros((hd, hd), F32)
                states[way, p] = jnp.concatenate([wi[way, 2 * p], second], axis=1).astype(BF16)

    for i in range(1, nh):
        token_copy(i, lax.rem(me + nh - i, nh)).wait_recv()

    @pl.when(not_first)
    def _():
        halo_copy(0).wait_recv()

    tail = halo[...].astype(F32)
    tail = [jnp.concatenate([tail[r * rim_rows + c:r * rim_rows + c + 1] for c in range(rim_rows)], axis=1)
            for r in range(rim_rows)]
    tail = jnp.concatenate([jnp.zeros((16 - rim_rows, depth), F32)] + tail, axis=0)
    if own % 16 == 0:
        for p in range(nh):
            xt[pl.ds(p * own, own), :] = xbuf[p]
    else:
        for p in range(nh):
            xs[pl.ds(p * own, own), :] = xbuf[p].astype(F32)
        xt[pl.ds(0, rows), :] = xs[pl.ds(0, rows), :].astype(BF16)
    xt[pl.ds(rows, LANES - 16 - rows), :] = jnp.zeros((LANES - 16 - rows, depth), BF16)
    xt[pl.ds(LANES - 16, 16), :] = tail.astype(BF16)

    gate[...] = jax.nn.sigmoid(mm_rows(lrwv[...], xt[...]))

    at_s = lax.broadcasted_iota(jnp.int32, (wide, wide), 0)
    at_t = lax.broadcasted_iota(jnp.int32, (wide, wide), 1)
    upper, left_half = at_s < hd, at_t < rows
    same = upper == left_half
    earlier = same & ((at_s // MB) < (at_t // MB))
    causal, anti = same & (at_s <= at_t), same & (at_s >= at_t)
    eye = (at_s == at_t).astype(F32)
    row_left = left_half[:1]

    def diagonal(a):
        return jnp.where(same, jnp.where(upper, a, pltpu.roll(a, rows, 1)), 0.0)

    def root_rate(p):
        first = gate[pl.ds(2 * p, 1), :] * lrb[2 * p]
        if 2 * p + 1 == heads:
            return jnp.sqrt(jnp.where(row_left, first, 0.0) / MB)
        second = gate[pl.ds(2 * p + 1, 1), :] * lrb[2 * p + 1]
        return jnp.sqrt(jnp.where(row_left, first, pltpu.roll(second, rows, 1)) / MB)

    def convolved(c):
        weights[c].wait()
        rounded = mm_rows(wv[c], xt[...]).astype(BF16).astype(F32)
        if inner < pairs * wide:
            row = lax.broadcasted_iota(jnp.int32, rounded.shape, 0)
            rounded = jnp.where(row < inner, rounded, 0.0)
        if c == 2:
            return rounded
        taps = taps_ref[...]
        total = taps[:, c * KERNEL + KERNEL - 1:c * KERNEL + KERNEL] * rounded
        for p in range(KERNEL - 1):
            at = c * KERNEL + p
            total = total + taps[:, at:at + 1] * pltpu.roll(rounded, KERNEL - 1 - p, 1)
        return total

    q_all, k_all, v_all = [convolved(c) for c in range(3)]
    each = range(pairs)
    part = [slice(j * wide, (j + 1) * wide) for j in each]
    root = [root_rate(j) for j in each]
    q = [diagonal(q_all[s]) for s in part]
    k = [diagonal(k_all[s]) for s in part]
    k = [k[j] * (root[j] * lax.rsqrt(jnp.sum(k[j] * k[j], axis=0, keepdims=True)
                                     + EPSILON * hd)) for j in each]
    v = [(diagonal(v_all[part[j]]) * root[j]).astype(BF16) for j in each]
    kt = [a.T.astype(BF16) for a in k]
    kb = [a.astype(BF16) for a in k]
    qb = [a.astype(BF16) for a in q]
    gram = [mm(kt[j], jnp.concatenate([kb[j], qb[j]], axis=1)) for j in each]
    one = [jnp.where(earlier, a[:, :wide], 0.0) for a in gram]
    oneb = [a.astype(BF16) for a in one]
    two = [mm(a, a) for a in oneb]
    three = [mm(oneb[j], two[j].astype(BF16)) for j in each]
    inv = [eye - one[j] + two[j] - three[j] for j in each]
    both = [jnp.concatenate([a, a.T], axis=1).astype(BF16) for a in inv]
    kv = [mm(jnp.concatenate([kb[j], v[j]], axis=0), both[j]) for j in each]
    for way, mask in ((0, causal), (1, anti)):
        lhs = [a[:, way * wide:(way + 1) * wide].astype(BF16) for a in kv]
        rhs = [jnp.concatenate(
            [kt[j], jnp.where(mask, gram[j][:, wide:], 0.0).astype(BF16)], axis=1) for j in each]
        made = [mm(lhs[j], rhs[j]) for j in each]
        for j in each:
            p = j
            maps[way, p, :, pl.ds(0, wide)] = (-made[j][:wide, :wide]).astype(BF16)
            maps[way, p, :, pl.ds(wide, wide)] = (q[j] - made[j][:wide, wide:]).astype(BF16)
            adds[way, p] = made[j][wide:wide + hd] + made[j][wide + hd:]

    def state_copy(way, gi):
        span = pl.ds(gi * pair_group, pair_group)
        return pltpu.make_async_remote_copy(
            src_ref=sending.at[way, span], dst_ref=states.at[way, span],
            send_sem=rsend.at[way, gi], recv_sem=rrecv.at[way, gi],
            device_id=(g + 1 - 2 * way, me), device_id_type=MESH)

    ways, normed = [], []
    for d in range(2):
        way = jnp.where(g < n // 2, d, 1 - d)
        starts = jnp.where(way == 0, g, n - 1 - g) == 0
        ends = jnp.where(way == 0, n - 1 - g, g) == 0
        ways.append((way, ends))
        for gi in range(groups):
            @pl.when(jnp.logical_not(starts))
            def _():
                state_copy(way, gi).wait_recv()

            mine = range(gi * pair_group, (gi + 1) * pair_group)
            old = [states[way, p] for p in mine]
            new = [mm(a, maps[way, p]) + adds[way, p] for a, p in zip(old, mine)]
            for a, b, p in zip(old, new, mine):
                sending[way, p] = (a.astype(F32) + b[:, :wide]).astype(BF16)

            @pl.when(jnp.logical_not(ends))
            def _():
                state_copy(way, gi).start()

            for b, p in zip(new, mine):
                reach[p] = b[:, wide:]

        for p in range(pairs):
            got = reach[p]
            centred = got - jnp.mean(got, axis=0, keepdims=True)
            spread = jnp.mean(centred * centred, axis=0, keepdims=True)
            scaled = centred * lax.rsqrt(spread + EPSILON)
            if d == 0:
                kept[p] = scaled
            else:
                normed.append(scaled + kept[p])

    turned = [a.T for a in normed]
    hidden = jnp.concatenate(
        [jnp.concatenate([a[:rows], a[rows:]], axis=1) for a in turned], axis=1)
    hidden = hidden[:, :inner].astype(BF16)
    out_weight.wait()

    def share_copy(j, i, to, slot):
        cols = pl.ds(j * (depth // chunks), depth // chunks)
        return pltpu.make_async_remote_copy(
            src_ref=pbuf.at[to, :, cols], dst_ref=rbuf.at[slot, :, cols],
            send_sem=psend.at[j, i], recv_sem=precv.at[j, i],
            device_id=(g, to), device_id_type=MESH)

    for j in range(chunks):
        cols = pl.ds(j * (depth // chunks), depth // chunks)
        share = mm(hidden, wov[:, cols])
        for p in range(nh):
            pbuf[p, :, cols] = share[p * own:(p + 1) * own].astype(BF16)
        for i in range(1, nh):
            share_copy(j, i, lax.rem(me + i, nh), me).start()

    for j in range(chunks):
        cols = pl.ds(j * (depth // chunks), depth // chunks)
        total = pbuf[me, :, cols].astype(F32)
        for i in range(1, nh):
            sender = lax.rem(me + nh - i, nh)
            share_copy(j, i, lax.rem(me + i, nh), sender).wait_recv()
            total = total + rbuf[sender, :, cols].astype(F32)
        out[:, cols] = total.astype(BF16)

    for i in range(1, nh):
        token_copy(i, me).wait_send()
        for j in range(chunks):
            share_copy(j, i, lax.rem(me + i, nh), me).wait_send()

    @pl.when(last_head & not_last)
    def _():
        for h in range(nh):
            halo_copy(h).wait_send()

    for way, ends in ways:
        @pl.when(jnp.logical_not(ends))
        def _():
            for gi in range(groups):
                state_copy(way, gi).wait_send()


def shards(n, nh, tokens, w_qkv, lr_weight, lr_base, conv_weight, w_init, w_out):
    own, depth = tokens.shape
    heads, hd = w_init.shape[1], w_init.shape[2]
    inner = heads * hd
    rows = own * nh
    pairs = (heads + 1) // 2
    padded = pairs * 2 * hd
    pair_group = 2 if pairs % 2 == 0 else 1
    groups = pairs // pair_group
    chunks = 2
    wide = 2 * hd
    hbm = pl.BlockSpec(memory_space=pltpu.HBM)
    smem = pl.BlockSpec(memory_space=pltpu.SMEM)
    dma = pltpu.SemaphoreType.DMA
    return pl.pallas_call(
        functools.partial(layer, (n, nh, heads, hd, pair_group, chunks)),
        out_shape=jax.ShapeDtypeStruct((own, depth), BF16),
        in_specs=[hbm, hbm, hbm, smem, hbm, hbm, hbm],
        out_specs=pl.BlockSpec(memory_space=pltpu.VMEM),
        scratch_shapes=[
            pltpu.VMEM((nh, own, depth), BF16),
            pltpu.VMEM((16, depth // (KERNEL - 1)), BF16),
            pltpu.VMEM((16, depth // (KERNEL - 1)), BF16),
            pltpu.VMEM((rows, depth) if own % 16 else (8, LANES), F32),
            pltpu.VMEM((LANES, depth), BF16),
            pltpu.VMEM((3, padded, depth), BF16),
            pltpu.VMEM(w_out.shape, BF16),
            pltpu.VMEM(lr_weight.shape, BF16),
            pltpu.VMEM(conv_weight.shape, F32),
            pltpu.VMEM((LANES, padded), F32),
            pltpu.VMEM((padded, LANES), F32),
            pltpu.VMEM(w_init.shape, F32),
            pltpu.VMEM((heads, LANES), F32),
            pltpu.VMEM((2, pairs, wide, 2 * wide), BF16),
            pltpu.VMEM((2, pairs, hd, 2 * wide), F32),
            pltpu.VMEM((2, pairs, hd, wide), BF16),
            pltpu.VMEM((2, pairs, hd, wide), BF16),
            pltpu.VMEM((pairs, hd, wide), F32),
            pltpu.VMEM((pairs, hd, wide), F32),
            pltpu.VMEM((nh, own, depth), BF16),
            pltpu.VMEM((nh, own, depth), BF16),
            dma((5,)),
            dma((3,)),
            dma((nh,)),
            dma((nh,)),
            dma((nh,)),
            dma((1,)),
            dma((2, groups)),
            dma((2, groups)),
            dma((chunks, nh)),
            dma((chunks, nh)),
        ],
        compiler_params=pltpu.CompilerParams(
            collective_id=0, has_side_effects=True, vmem_limit_bytes=48 * 2 ** 20),
    )(tokens, w_qkv, lr_weight, lr_base, conv_weight, w_init, w_out)


def solution(mesh):
    placed = (
        P(("seq", "head"), None),
        P(None, "head", None),
        P("head", None),
        P("head"),
        P(None, None, "head"),
        P(None, "head", None, None),
        P("head", None),
    )
    return jax.shard_map(
        functools.partial(shards, mesh.shape["seq"], mesh.shape["head"]),
        mesh=mesh, in_specs=placed, out_specs=P(("seq", "head"), None), check_vma=False
    )
```

```python
import functools

import jax
import jax.numpy as jnp
from jax import lax
from jax.experimental import pallas as pl
from jax.experimental.pallas import tpu as pltpu
from jax.sharding import PartitionSpec as P

MB = 16
KERNEL = 4
EPSILON = 1e-05
LANES = 128
MESH = pl.DeviceIdType.MESH
F32, BF16 = jnp.float32, jnp.bfloat16


def mm(a, b):
    return jnp.dot(a, b, preferred_element_type=F32)


def mm_rows(a, b):
    return lax.dot_general(a, b, (((1,), (1,)), ((), ())), preferred_element_type=F32)


def layer(cfg, tok, wqkv, lrw, lrb, cw, winit, wout, out,
          xbuf, rim, halo, xs, xt, wv, wov, lrwv, cwv, cwt, taps_ref, wi, gate,
          maps, adds, states, sending, reach, kept, given, taken, pbuf, rbuf,
          lsem, wsem, tsend, trecv, hsend, hrecv, gsend, grecv, rsend, rrecv, psend, precv):
    n, nh, heads, hd, pair_group, chunks = cfg
    own, depth = tok.shape
    rows = own * nh
    inner = heads * hd
    pairs = (heads + 1) // 2
    groups = pairs // pair_group
    wide = 2 * hd
    g, me = lax.axis_index("seq"), lax.axis_index("head")
    not_first, not_last = g > 0, g < n - 1
    core, chip, chips = lax.rem(g, 2), g // 2, n // 2
    other = g + 1 - 2 * core
    chip_before, chip_after = chip > 0, chip < chips - 1
    last_head = me == nh - 1

    small = [pltpu.make_async_copy(a, b, lsem.at[k]) for k, (a, b) in enumerate((
        (tok, xbuf.at[me]), (lrw, lrwv), (cw, cwv), (winit, wi)))]
    for copy in small:
        copy.start()
    weights = []
    for c in range(3):
        weights.append(pltpu.make_async_copy(wqkv.at[c], wv.at[c, pl.ds(0, inner)], wsem.at[c]))
        weights[c].start()
    out_weight = pltpu.make_async_copy(wout, wov, lsem.at[4])
    out_weight.start()

    barrier = pltpu.get_barrier_semaphore()
    for i in range(1, nh):
        pl.semaphore_signal(barrier, inc=1, device_id=(g, lax.rem(me + i, nh)), device_id_type=MESH)

    @pl.when(not_first)
    def _():
        pl.semaphore_signal(barrier, inc=1, device_id=(g - 1, nh - 1), device_id_type=MESH)

    pl.semaphore_signal(barrier, inc=1, device_id=(other, me), device_id_type=MESH)

    @pl.when(chip_before)
    def _():
        pl.semaphore_signal(barrier, inc=1, device_id=(2 * chip - 1, me), device_id_type=MESH)

    @pl.when(chip_after)
    def _():
        pl.semaphore_signal(barrier, inc=1, device_id=(2 * chip + 2, me), device_id_type=MESH)

    relays_on = jnp.where(core == 1, chip_after, chip_before)
    pl.semaphore_wait(barrier, nh + jnp.where(relays_on, 2, 0)
                      + jnp.where(last_head & not_last, nh, 0))

    def token_copy(i, slot):
        return pltpu.make_async_remote_copy(
            src_ref=tok, dst_ref=xbuf.at[slot], send_sem=tsend.at[i], recv_sem=trecv.at[i],
            device_id=(g, lax.rem(me + i, nh)), device_id_type=MESH)

    def halo_copy(h):
        return pltpu.make_async_remote_copy(
            src_ref=rim, dst_ref=halo, send_sem=hsend.at[h], recv_sem=hrecv.at[0],
            device_id=(g + 1, h), device_id_type=MESH)

    for i in range(1, nh):
        token_copy(i, me).start()

    small[0].wait()
    rim_rows = KERNEL - 1
    piece = depth // rim_rows
    mine_last = xbuf[me].astype(F32)[own - rim_rows:]
    rim[...] = jnp.concatenate(
        [mine_last[r:r + 1, c * piece:(c + 1) * piece] for r in range(rim_rows) for c in range(rim_rows)]
        + [jnp.zeros((rim.shape[0] - rim_rows * rim_rows, piece), F32)], axis=0).astype(BF16)

    @pl.when(last_head & not_last)
    def _():
        for h in range(nh):
            halo_copy(h).start()

    @pl.when(jnp.logical_not(not_first))
    def _():
        halo[...] = jnp.zeros_like(halo)

    for copy in small[1:]:
        copy.wait()

    cwt[...] = jnp.zeros_like(cwt)
    for c in range(2):
        cwt[pl.ds(c * KERNEL, KERNEL), pl.ds(0, inner)] = cwv[c]
    for j in range(pairs):
        taps_ref[pl.ds(j * LANES, LANES), :] = cwt[:, pl.ds(j * LANES, LANES)].T

    for way, outer in ((0, jnp.logical_not(chip_before)), (1, jnp.logical_not(chip_after))):
        @pl.when(outer)
        def _():
            for p in range(pairs):
                second = wi[way, 2 * p + 1] if 2 * p + 1 < heads else jnp.zeros((hd, hd), F32)
                states[way, p] = jnp.concatenate([wi[way, 2 * p], second], axis=1).astype(BF16)

    for i in range(1, nh):
        token_copy(i, lax.rem(me + nh - i, nh)).wait_recv()

    @pl.when(not_first)
    def _():
        halo_copy(0).wait_recv()

    tail = halo[...].astype(F32)
    tail = [jnp.concatenate([tail[r * rim_rows + c:r * rim_rows + c + 1] for c in range(rim_rows)], axis=1)
            for r in range(rim_rows)]
    tail = jnp.concatenate([jnp.zeros((16 - rim_rows, depth), F32)] + tail, axis=0)
    if own % 16 == 0:
        for p in range(nh):
            xt[pl.ds(p * own, own), :] = xbuf[p]
    else:
        for p in range(nh):
            xs[pl.ds(p * own, own), :] = xbuf[p].astype(F32)
        xt[pl.ds(0, rows), :] = xs[pl.ds(0, rows), :].astype(BF16)
    xt[pl.ds(rows, LANES - 16 - rows), :] = jnp.zeros((LANES - 16 - rows, depth), BF16)
    xt[pl.ds(LANES - 16, 16), :] = tail.astype(BF16)

    gate[...] = jax.nn.sigmoid(mm_rows(lrwv[...], xt[...]))

    at_s = lax.broadcasted_iota(jnp.int32, (wide, wide), 0)
    at_t = lax.broadcasted_iota(jnp.int32, (wide, wide), 1)
    upper, left_half = at_s < hd, at_t < rows
    same = upper == left_half
    earlier = same & ((at_s // MB) < (at_t // MB))
    causal, anti = same & (at_s <= at_t), same & (at_s >= at_t)
    eye = (at_s == at_t).astype(F32)
    row_left = left_half[:1]

    def diagonal(a):
        return jnp.where(same, jnp.where(upper, a, pltpu.roll(a, rows, 1)), 0.0)

    def root_rate(p):
        first = gate[pl.ds(2 * p, 1), :] * lrb[2 * p]
        if 2 * p + 1 == heads:
            return jnp.sqrt(jnp.where(row_left, first, 0.0) / MB)
        second = gate[pl.ds(2 * p + 1, 1), :] * lrb[2 * p + 1]
        return jnp.sqrt(jnp.where(row_left, first, pltpu.roll(second, rows, 1)) / MB)

    def convolved(c):
        weights[c].wait()
        rounded = mm_rows(wv[c], xt[...]).astype(BF16).astype(F32)
        if inner < pairs * wide:
            row = lax.broadcasted_iota(jnp.int32, rounded.shape, 0)
            rounded = jnp.where(row < inner, rounded, 0.0)
        if c == 2:
            return rounded
        taps = taps_ref[...]
        total = taps[:, c * KERNEL + KERNEL - 1:c * KERNEL + KERNEL] * rounded
        for p in range(KERNEL - 1):
            at = c * KERNEL + p
            total = total + taps[:, at:at + 1] * pltpu.roll(rounded, KERNEL - 1 - p, 1)
        return total

    q_all, k_all, v_all = [convolved(c) for c in range(3)]
    each = range(pairs)
    part = [slice(j * wide, (j + 1) * wide) for j in each]
    root = [root_rate(j) for j in each]
    q = [diagonal(q_all[s]) for s in part]
    k = [diagonal(k_all[s]) for s in part]
    k = [k[j] * (root[j] * lax.rsqrt(jnp.sum(k[j] * k[j], axis=0, keepdims=True)
                                     + EPSILON * hd)) for j in each]
    v = [(diagonal(v_all[part[j]]) * root[j]).astype(BF16) for j in each]
    kt = [a.T.astype(BF16) for a in k]
    kb = [a.astype(BF16) for a in k]
    qb = [a.astype(BF16) for a in q]
    gram = [mm(kt[j], jnp.concatenate([kb[j], qb[j]], axis=1)) for j in each]
    one = [jnp.where(earlier, a[:, :wide], 0.0) for a in gram]
    oneb = [a.astype(BF16) for a in one]
    two = [mm(a, a) for a in oneb]
    three = [mm(oneb[j], two[j].astype(BF16)) for j in each]
    inv = [eye - one[j] + two[j] - three[j] for j in each]
    both = [jnp.concatenate([a, a.T], axis=1).astype(BF16) for a in inv]
    kv = [mm(jnp.concatenate([kb[j], v[j]], axis=0), both[j]) for j in each]
    for way, mask in ((0, causal), (1, anti)):
        lhs = [a[:, way * wide:(way + 1) * wide].astype(BF16) for a in kv]
        rhs = [jnp.concatenate(
            [kt[j], jnp.where(mask, gram[j][:, wide:], 0.0).astype(BF16)], axis=1) for j in each]
        made = [mm(lhs[j], rhs[j]) for j in each]
        for j in each:
            p = j
            step = (-made[j][:wide, :wide]).astype(BF16)
            maps[way, p, :, pl.ds(0, wide)] = step
            given[way, p, pl.ds(0, wide), :] = step
            maps[way, p, :, pl.ds(wide, wide)] = (q[j] - made[j][:wide, wide:]).astype(BF16)
            shift = made[j][wide:wide + hd] + made[j][wide + hd:]
            adds[way, p] = shift
            given[way, p, pl.ds(wide, hd), :] = shift[:, :wide].astype(BF16)

    def map_copy(gi):
        span = pl.ds(gi * pair_group, pair_group)
        return pltpu.make_async_remote_copy(
            src_ref=given.at[core, span], dst_ref=taken.at[span],
            send_sem=gsend.at[gi], recv_sem=grecv.at[gi],
            device_id=(other, me), device_id_type=MESH)

    for gi in range(groups):
        map_copy(gi).start()
    relay = 1 - core
    for gi in range(groups):
        map_copy(gi).wait_recv()
        mine = range(gi * pair_group, (gi + 1) * pair_group)
        first = [taken[p] for p in mine]
        then = [mm(a, maps[relay, p]) for a, p in zip(first, mine)]
        for a, b, p in zip(first, then, mine):
            a = a.astype(F32)
            near, far = pl.ds(0, wide), pl.ds(wide, wide)
            maps[relay, p, :, near] = (maps[relay, p, :, near].astype(F32) + a[:wide]
                                       + b[:wide, :wide]).astype(BF16)
            maps[relay, p, :, far] = (maps[relay, p, :, far].astype(F32)
                                      + b[:wide, wide:]).astype(BF16)
            adds[relay, p, :, near] = adds[relay, p, :, near] + a[wide:] + b[wide:, :wide]
            adds[relay, p, :, far] = adds[relay, p, :, far] + b[wide:, wide:]

    def state_copy(way, gi, hop):
        span = pl.ds(gi * pair_group, pair_group)
        return pltpu.make_async_remote_copy(
            src_ref=sending.at[span], dst_ref=states.at[way, span],
            send_sem=rsend.at[gi, hop - 1], recv_sem=rrecv.at[way, gi],
            device_id=(g + hop * (1 - 2 * way), me), device_id_type=MESH)

    normed = []
    for d in range(2):
        way = jnp.where(g < n // 2, d, 1 - d)
        starts = jnp.where(way == 0, chip, chips - 1 - chip) == 0
        onward = (way == relay) & relays_on
        for gi in range(groups):
            @pl.when(jnp.logical_not(starts))
            def _():
                state_copy(way, gi, 1).wait_recv()

            mine = range(gi * pair_group, (gi + 1) * pair_group)
            old = [states[way, p] for p in mine]
            new = [mm(a, maps[way, p]) + adds[way, p] for a, p in zip(old, mine)]

            @pl.when(onward)
            def _():
                for a, b, p in zip(old, new, mine):
                    sending[p] = (a.astype(F32) + b[:, :wide]).astype(BF16)
                state_copy(way, gi, 2).start()
                state_copy(way, gi, 1).start()

            for b, p in zip(new, mine):
                reach[p] = b[:, wide:]

        for p in range(pairs):
            got = reach[p]
            centred = got - jnp.mean(got, axis=0, keepdims=True)
            spread = jnp.mean(centred * centred, axis=0, keepdims=True)
            scaled = centred * lax.rsqrt(spread + EPSILON)
            if d == 0:
                kept[p] = scaled
            else:
                normed.append(scaled + kept[p])

    turned = [a.T for a in normed]
    hidden = jnp.concatenate(
        [jnp.concatenate([a[:rows], a[rows:]], axis=1) for a in turned], axis=1)
    hidden = hidden[:, :inner].astype(BF16)
    out_weight.wait()

    def share_copy(j, i, to, slot):
        cols = pl.ds(j * (depth // chunks), depth // chunks)
        return pltpu.make_async_remote_copy(
            src_ref=pbuf.at[to, :, cols], dst_ref=rbuf.at[slot, :, cols],
            send_sem=psend.at[j, i], recv_sem=precv.at[j, i],
            device_id=(g, to), device_id_type=MESH)

    for j in range(chunks):
        cols = pl.ds(j * (depth // chunks), depth // chunks)
        share = mm(hidden, wov[:, cols])
        for p in range(nh):
            pbuf[p, :, cols] = share[p * own:(p + 1) * own].astype(BF16)
        for i in range(1, nh):
            share_copy(j, i, lax.rem(me + i, nh), me).start()

    for j in range(chunks):
        cols = pl.ds(j * (depth // chunks), depth // chunks)
        total = pbuf[me, :, cols].astype(F32)
        for i in range(1, nh):
            sender = lax.rem(me + nh - i, nh)
            share_copy(j, i, lax.rem(me + i, nh), sender).wait_recv()
            total = total + rbuf[sender, :, cols].astype(F32)
        out[:, cols] = total.astype(BF16)

    for i in range(1, nh):
        token_copy(i, me).wait_send()
        for j in range(chunks):
            share_copy(j, i, lax.rem(me + i, nh), me).wait_send()

    @pl.when(last_head & not_last)
    def _():
        for h in range(nh):
            halo_copy(h).wait_send()

    for gi in range(groups):
        map_copy(gi).wait_send()

    @pl.when(relays_on)
    def _():
        for gi in range(groups):
            for hop in (1, 2):
                state_copy(relay, gi, hop).wait_send()


def shards(n, nh, tokens, w_qkv, lr_weight, lr_base, conv_weight, w_init, w_out):
    own, depth = tokens.shape
    heads, hd = w_init.shape[1], w_init.shape[2]
    inner = heads * hd
    rows = own * nh
    pairs = (heads + 1) // 2
    padded = pairs * 2 * hd
    pair_group = 2 if pairs % 2 == 0 else 1
    groups = pairs // pair_group
    chunks = 2
    wide = 2 * hd
    hbm = pl.BlockSpec(memory_space=pltpu.HBM)
    smem = pl.BlockSpec(memory_space=pltpu.SMEM)
    dma = pltpu.SemaphoreType.DMA
    return pl.pallas_call(
        functools.partial(layer, (n, nh, heads, hd, pair_group, chunks)),
        out_shape=jax.ShapeDtypeStruct((own, depth), BF16),
        in_specs=[hbm, hbm, hbm, smem, hbm, hbm, hbm],
        out_specs=pl.BlockSpec(memory_space=pltpu.VMEM),
        scratch_shapes=[
            pltpu.VMEM((nh, own, depth), BF16),
            pltpu.VMEM((16, depth // (KERNEL - 1)), BF16),
            pltpu.VMEM((16, depth // (KERNEL - 1)), BF16),
            pltpu.VMEM((rows, depth) if own % 16 else (8, LANES), F32),
            pltpu.VMEM((LANES, depth), BF16),
            pltpu.VMEM((3, padded, depth), BF16),
            pltpu.VMEM(w_out.shape, BF16),
            pltpu.VMEM(lr_weight.shape, BF16),
            pltpu.VMEM(conv_weight.shape, F32),
            pltpu.VMEM((LANES, padded), F32),
            pltpu.VMEM((padded, LANES), F32),
            pltpu.VMEM(w_init.shape, F32),
            pltpu.VMEM((heads, LANES), F32),
            pltpu.VMEM((2, pairs, wide, 2 * wide), BF16),
            pltpu.VMEM((2, pairs, hd, 2 * wide), F32),
            pltpu.VMEM((2, pairs, hd, wide), BF16),
            pltpu.VMEM((pairs, hd, wide), BF16),
            pltpu.VMEM((pairs, hd, wide), F32),
            pltpu.VMEM((pairs, hd, wide), F32),
            pltpu.VMEM((2, pairs, wide + hd, wide), BF16),
            pltpu.VMEM((pairs, wide + hd, wide), BF16),
            pltpu.VMEM((nh, own, depth), BF16),
            pltpu.VMEM((nh, own, depth), BF16),
            dma((5,)),
            dma((3,)),
            dma((nh,)),
            dma((nh,)),
            dma((nh,)),
            dma((1,)),
            dma((groups,)),
            dma((groups,)),
            dma((groups, 2)),
            dma((2, groups)),
            dma((chunks, nh)),
            dma((chunks, nh)),
        ],
        compiler_params=pltpu.CompilerParams(
            collective_id=0, has_side_effects=True, vmem_limit_bytes=60 * 2 ** 20),
    )(tokens, w_qkv, lr_weight, lr_base, conv_weight, w_init, w_out)


def solution(mesh):
    placed = (
        P(("seq", "head"), None),
        P(None, "head", None),
        P("head", None),
        P("head"),
        P(None, None, "head"),
        P(None, "head", None, None),
        P("head", None),
    )
    return jax.shard_map(
        functools.partial(shards, mesh.shape["seq"], mesh.shape["head"]),
        mesh=mesh, in_specs=placed, out_specs=P(("seq", "head"), None), check_vma=False
    )
```

```python
import functools

import jax
import jax.numpy as jnp
from jax import lax
from jax.experimental import pallas as pl
from jax.experimental.pallas import tpu as pltpu
from jax.sharding import PartitionSpec as P

MB = 16
KERNEL = 4
EPSILON = 1e-05
LANES = 128
MESH = pl.DeviceIdType.MESH
F32, BF16 = jnp.float32, jnp.bfloat16


def mm(a, b):
    return jnp.dot(a, b, preferred_element_type=F32)


def mm_rows(a, b):
    return lax.dot_general(a, b, (((1,), (1,)), ((), ())), preferred_element_type=F32)


def layer(cfg, tok, wqkv, lrw, lrb, cw, winit, wout, shares,
          xbuf, rim, halo, xs, xt, wv, wov, lrwv, cwv, cwt, taps_ref, wi, gate,
          maps, adds, states, sending, reach, kept, given, taken, pbuf,
          lsem, wsem, tsend, trecv, hsend, hrecv, gsend, grecv, rsend, rrecv, psend, precv):
    n, nh, heads, hd, pair_group, chunks = cfg
    own, depth = tok.shape
    rows = own * nh
    inner = heads * hd
    pairs = (heads + 1) // 2
    groups = pairs // pair_group
    wide = 2 * hd
    g, me = lax.axis_index("seq"), lax.axis_index("head")
    not_first, not_last = g > 0, g < n - 1
    core, chip, chips = lax.rem(g, 2), g // 2, n // 2
    other = g + 1 - 2 * core
    chip_before, chip_after = chip > 0, chip < chips - 1
    last_head = me == nh - 1

    small = [pltpu.make_async_copy(a, b, lsem.at[k]) for k, (a, b) in enumerate((
        (tok, xbuf.at[me]), (lrw, lrwv), (cw, cwv), (winit, wi)))]
    for copy in small:
        copy.start()
    weights = []
    for c in range(3):
        weights.append(pltpu.make_async_copy(wqkv.at[c], wv.at[c, pl.ds(0, inner)], wsem.at[c]))
        weights[c].start()
    out_weight = pltpu.make_async_copy(wout, wov, lsem.at[4])

    barrier = pltpu.get_barrier_semaphore()
    for i in range(1, nh):
        pl.semaphore_signal(barrier, inc=1, device_id=(g, lax.rem(me + i, nh)), device_id_type=MESH)

    @pl.when(not_first)
    def _():
        pl.semaphore_signal(barrier, inc=1, device_id=(g - 1, nh - 1), device_id_type=MESH)

    pl.semaphore_signal(barrier, inc=1, device_id=(other, me), device_id_type=MESH)

    @pl.when(chip_before & (core == 1))
    def _():
        pl.semaphore_signal(barrier, inc=1, device_id=(2 * chip - 2 + core, me), device_id_type=MESH)

    @pl.when(chip_after & (core == 0))
    def _():
        pl.semaphore_signal(barrier, inc=1, device_id=(2 * chip + 2 + core, me), device_id_type=MESH)

    relays_on = jnp.where(core == 1, chip_after, chip_before)
    pl.semaphore_wait(barrier, nh + jnp.where(relays_on, 1, 0)
                      + jnp.where(last_head & not_last, nh, 0))

    def token_copy(i, slot):
        return pltpu.make_async_remote_copy(
            src_ref=tok, dst_ref=xbuf.at[slot], send_sem=tsend.at[i], recv_sem=trecv.at[i],
            device_id=(g, lax.rem(me + i, nh)), device_id_type=MESH)

    def halo_copy(h):
        return pltpu.make_async_remote_copy(
            src_ref=rim, dst_ref=halo, send_sem=hsend.at[h], recv_sem=hrecv.at[0],
            device_id=(g + 1, h), device_id_type=MESH)

    for i in range(1, nh):
        token_copy(i, me).start()

    small[0].wait()
    rim_rows = KERNEL - 1
    piece = depth // rim_rows
    mine_last = xbuf[me].astype(F32)[own - rim_rows:]
    rim[...] = jnp.concatenate(
        [mine_last[r:r + 1, c * piece:(c + 1) * piece] for r in range(rim_rows) for c in range(rim_rows)]
        + [jnp.zeros((rim.shape[0] - rim_rows * rim_rows, piece), F32)], axis=0).astype(BF16)

    @pl.when(last_head & not_last)
    def _():
        for h in range(nh):
            halo_copy(h).start()

    @pl.when(jnp.logical_not(not_first))
    def _():
        halo[...] = jnp.zeros_like(halo)

    for copy in small[1:]:
        copy.wait()

    cwt[...] = jnp.zeros_like(cwt)
    for c in range(2):
        cwt[pl.ds(c * KERNEL, KERNEL), pl.ds(0, inner)] = cwv[c]
    for j in range(pairs):
        taps_ref[pl.ds(j * LANES, LANES), :] = cwt[:, pl.ds(j * LANES, LANES)].T

    for way, outer in ((0, jnp.logical_not(chip_before)), (1, jnp.logical_not(chip_after))):
        @pl.when(outer)
        def _():
            for p in range(pairs):
                second = wi[way, 2 * p + 1] if 2 * p + 1 < heads else jnp.zeros((hd, hd), F32)
                states[way, p] = jnp.concatenate([wi[way, 2 * p], second], axis=1).astype(BF16)

    for i in range(1, nh):
        token_copy(i, lax.rem(me + nh - i, nh)).wait_recv()

    @pl.when(not_first)
    def _():
        halo_copy(0).wait_recv()

    tail = halo[...].astype(F32)
    tail = [jnp.concatenate([tail[r * rim_rows + c:r * rim_rows + c + 1] for c in range(rim_rows)], axis=1)
            for r in range(rim_rows)]
    tail = jnp.concatenate([jnp.zeros((16 - rim_rows, depth), F32)] + tail, axis=0)
    if own % 16 == 0:
        for p in range(nh):
            xt[pl.ds(p * own, own), :] = xbuf[p]
    else:
        for p in range(nh):
            xs[pl.ds(p * own, own), :] = xbuf[p].astype(F32)
        xt[pl.ds(0, rows), :] = xs[pl.ds(0, rows), :].astype(BF16)
    xt[pl.ds(rows, LANES - 16 - rows), :] = jnp.zeros((LANES - 16 - rows, depth), BF16)
    xt[pl.ds(LANES - 16, 16), :] = tail.astype(BF16)

    gate[...] = jax.nn.sigmoid(mm_rows(lrwv[...], xt[...]))

    at_s = lax.broadcasted_iota(jnp.int32, (wide, wide), 0)
    at_t = lax.broadcasted_iota(jnp.int32, (wide, wide), 1)
    upper, left_half = at_s < hd, at_t < rows
    same = upper == left_half
    earlier = same & ((at_s // MB) < (at_t // MB))
    causal, anti = same & (at_s <= at_t), same & (at_s >= at_t)
    eye = (at_s == at_t).astype(F32)
    row_left = left_half[:1]

    def diagonal(a):
        return jnp.where(same, jnp.where(upper, a, pltpu.roll(a, rows, 1)), 0.0)

    def root_rate(p):
        first = gate[pl.ds(2 * p, 1), :] * lrb[2 * p]
        if 2 * p + 1 == heads:
            return jnp.sqrt(jnp.where(row_left, first, 0.0) / MB)
        second = gate[pl.ds(2 * p + 1, 1), :] * lrb[2 * p + 1]
        return jnp.sqrt(jnp.where(row_left, first, pltpu.roll(second, rows, 1)) / MB)

    def convolved(c):
        weights[c].wait()
        rounded = mm_rows(wv[c], xt[...]).astype(BF16).astype(F32)
        if inner < pairs * wide:
            row = lax.broadcasted_iota(jnp.int32, rounded.shape, 0)
            rounded = jnp.where(row < inner, rounded, 0.0)
        if c == 2:
            return rounded
        taps = taps_ref[...]
        total = taps[:, c * KERNEL + KERNEL - 1:c * KERNEL + KERNEL] * rounded
        for p in range(KERNEL - 1):
            at = c * KERNEL + p
            total = total + taps[:, at:at + 1] * pltpu.roll(rounded, KERNEL - 1 - p, 1)
        return total

    q_all, k_all, v_all = [convolved(c) for c in range(3)]
    out_weight.start()
    each = range(pairs)
    part = [slice(j * wide, (j + 1) * wide) for j in each]
    root = [root_rate(j) for j in each]
    q = [diagonal(q_all[s]) for s in part]
    k = [diagonal(k_all[s]) for s in part]
    k = [k[j] * (root[j] * lax.rsqrt(jnp.sum(k[j] * k[j], axis=0, keepdims=True)
                                     + EPSILON * hd)) for j in each]
    v = [(diagonal(v_all[part[j]]) * root[j]).astype(BF16) for j in each]
    kt = [a.T.astype(BF16) for a in k]
    kb = [a.astype(BF16) for a in k]
    qb = [a.astype(BF16) for a in q]
    gram = [mm(kt[j], jnp.concatenate([kb[j], qb[j]], axis=1)) for j in each]
    one = [jnp.where(earlier, a[:, :wide], 0.0) for a in gram]
    oneb = [a.astype(BF16) for a in one]
    two = [mm(a, a) for a in oneb]
    three = [mm(oneb[j], two[j].astype(BF16)) for j in each]
    inv = [eye - one[j] + two[j] - three[j] for j in each]
    both = [jnp.concatenate([a, a.T], axis=1).astype(BF16) for a in inv]
    kv = [mm(jnp.concatenate([kb[j], v[j]], axis=0), both[j]) for j in each]
    for way, mask in ((0, causal), (1, anti)):
        lhs = [a[:, way * wide:(way + 1) * wide].astype(BF16) for a in kv]
        rhs = [jnp.concatenate(
            [kt[j], jnp.where(mask, gram[j][:, wide:], 0.0).astype(BF16)], axis=1) for j in each]
        made = [mm(lhs[j], rhs[j]) for j in each]
        for j in each:
            p = j
            step = (-made[j][:wide, :wide]).astype(BF16)
            maps[way, p, :, pl.ds(0, wide)] = step
            given[way, p, pl.ds(0, wide), :] = step
            maps[way, p, :, pl.ds(wide, wide)] = (q[j] - made[j][:wide, wide:]).astype(BF16)
            shift = made[j][wide:wide + hd] + made[j][wide + hd:]
            adds[way, p] = shift
            given[way, p, pl.ds(wide, hd), :] = shift[:, :wide].astype(BF16)

    def map_copy(gi):
        span = pl.ds(gi * pair_group, pair_group)
        return pltpu.make_async_remote_copy(
            src_ref=given.at[core, span], dst_ref=taken.at[span],
            send_sem=gsend.at[gi], recv_sem=grecv.at[gi],
            device_id=(other, me), device_id_type=MESH)

    for gi in range(groups):
        map_copy(gi).start()
    relay = 1 - core
    for gi in range(groups):
        map_copy(gi).wait_recv()
        mine = range(gi * pair_group, (gi + 1) * pair_group)
        first = [taken[p] for p in mine]
        then = [mm(a, maps[relay, p]) for a, p in zip(first, mine)]
        for a, b, p in zip(first, then, mine):
            a = a.astype(F32)
            near, far = pl.ds(0, wide), pl.ds(wide, wide)
            maps[relay, p, :, near] = (maps[relay, p, :, near].astype(F32) + a[:wide]
                                       + b[:wide, :wide]).astype(BF16)
            maps[relay, p, :, far] = (maps[relay, p, :, far].astype(F32)
                                      + b[:wide, wide:]).astype(BF16)
            adds[relay, p, :, near] = adds[relay, p, :, near] + a[wide:] + b[wide:, :wide]
            adds[relay, p, :, far] = adds[relay, p, :, far] + b[wide:, wide:]

    def state_copy(way, gi):
        span = pl.ds(gi * pair_group, pair_group)
        return pltpu.make_async_remote_copy(
            src_ref=sending.at[span], dst_ref=states.at[way, span],
            send_sem=rsend.at[gi, 0], recv_sem=rrecv.at[way, gi],
            device_id=(g + 2 * (1 - 2 * way), me), device_id_type=MESH)

    def leaf_copy(way, gi):
        span = pl.ds(gi * pair_group, pair_group)
        return pltpu.make_async_remote_copy(
            src_ref=states.at[way, span], dst_ref=states.at[way, span],
            send_sem=rsend.at[gi, 1], recv_sem=rrecv.at[way, gi],
            device_id=(other, me), device_id_type=MESH)

    normed = []
    for d in range(2):
        way = jnp.where(g < n // 2, d, 1 - d)
        starts = jnp.where(way == 0, chip, chips - 1 - chip) == 0
        onward = (way == relay) & relays_on
        for gi in range(groups):
            @pl.when(jnp.logical_not(starts))
            def _():
                state_copy(way, gi).wait_recv()

            mine = range(gi * pair_group, (gi + 1) * pair_group)
            old = [states[way, p] for p in mine]
            new = [mm(a, maps[way, p]) + adds[way, p] for a, p in zip(old, mine)]

            @pl.when(onward)
            def _():
                for a, b, p in zip(old, new, mine):
                    sending[p] = (a.astype(F32) + b[:, :wide]).astype(BF16)
                state_copy(way, gi).start()

            @pl.when((way == relay) & jnp.logical_not(starts))
            def _():
                leaf_copy(way, gi).start()

            for b, p in zip(new, mine):
                reach[p] = b[:, wide:]

        for p in range(pairs):
            got = reach[p]
            centred = got - jnp.mean(got, axis=0, keepdims=True)
            spread = jnp.mean(centred * centred, axis=0, keepdims=True)
            scaled = centred * lax.rsqrt(spread + EPSILON)
            if d == 0:
                kept[p] = scaled
            else:
                normed.append(scaled + kept[p])

    turned = [a.T for a in normed]
    hidden = jnp.concatenate(
        [jnp.concatenate([a[:rows], a[rows:]], axis=1) for a in turned], axis=1)
    hidden = hidden[:, :inner].astype(BF16)
    out_weight.wait()

    def share_copy(j, i, to, slot):
        cols = pl.ds(j * (depth // chunks), depth // chunks)
        return pltpu.make_async_remote_copy(
            src_ref=pbuf.at[to, :, cols], dst_ref=shares.at[slot, :, cols],
            send_sem=psend.at[j, i], recv_sem=precv.at[j, i],
            device_id=(g, to), device_id_type=MESH)

    for j in range(chunks):
        cols = pl.ds(j * (depth // chunks), depth // chunks)
        share = mm(hidden, wov[:, cols])
        for p in range(nh):
            pbuf[p, :, cols] = share[p * own:(p + 1) * own].astype(BF16)
        for i in range(1, nh):
            share_copy(j, i, lax.rem(me + i, nh), me).start()

    kept_share = pltpu.make_async_copy(pbuf.at[me], shares.at[me], lsem.at[0])
    kept_share.start()
    for j in range(chunks):
        for i in range(1, nh):
            share_copy(j, i, lax.rem(me + i, nh), lax.rem(me + nh - i, nh)).wait_recv()
    kept_share.wait()

    for i in range(1, nh):
        token_copy(i, me).wait_send()
        for j in range(chunks):
            share_copy(j, i, lax.rem(me + i, nh), me).wait_send()

    @pl.when(last_head & not_last)
    def _():
        for h in range(nh):
            halo_copy(h).wait_send()

    for gi in range(groups):
        map_copy(gi).wait_send()

    @pl.when(relays_on)
    def _():
        for gi in range(groups):
            state_copy(relay, gi).wait_send()

    @pl.when(jnp.where(core == 1, chip_before, chip_after))
    def _():
        for gi in range(groups):
            leaf_copy(relay, gi).wait_send()


def shards(n, nh, tokens, w_qkv, lr_weight, lr_base, conv_weight, w_init, w_out):
    own, depth = tokens.shape
    heads, hd = w_init.shape[1], w_init.shape[2]
    inner = heads * hd
    rows = own * nh
    pairs = (heads + 1) // 2
    padded = pairs * 2 * hd
    pair_group = 2 if pairs % 2 == 0 else 1
    groups = pairs // pair_group
    chunks = 2
    wide = 2 * hd
    hbm = pl.BlockSpec(memory_space=pltpu.HBM)
    smem = pl.BlockSpec(memory_space=pltpu.SMEM)
    dma = pltpu.SemaphoreType.DMA
    shares = pl.pallas_call(
        functools.partial(layer, (n, nh, heads, hd, pair_group, chunks)),
        out_shape=jax.ShapeDtypeStruct((nh, own, depth), BF16),
        in_specs=[hbm, hbm, hbm, smem, hbm, hbm, hbm],
        out_specs=hbm,
        scratch_shapes=[
            pltpu.VMEM((nh, own, depth), BF16),
            pltpu.VMEM((16, depth // (KERNEL - 1)), BF16),
            pltpu.VMEM((16, depth // (KERNEL - 1)), BF16),
            pltpu.VMEM((rows, depth) if own % 16 else (8, LANES), F32),
            pltpu.VMEM((LANES, depth), BF16),
            pltpu.VMEM((3, padded, depth), BF16),
            pltpu.VMEM(w_out.shape, BF16),
            pltpu.VMEM(lr_weight.shape, BF16),
            pltpu.VMEM(conv_weight.shape, F32),
            pltpu.VMEM((LANES, padded), F32),
            pltpu.VMEM((padded, LANES), F32),
            pltpu.VMEM(w_init.shape, F32),
            pltpu.VMEM((heads, LANES), F32),
            pltpu.VMEM((2, pairs, wide, 2 * wide), BF16),
            pltpu.VMEM((2, pairs, hd, 2 * wide), F32),
            pltpu.VMEM((2, pairs, hd, wide), BF16),
            pltpu.VMEM((pairs, hd, wide), BF16),
            pltpu.VMEM((pairs, hd, wide), F32),
            pltpu.VMEM((pairs, hd, wide), F32),
            pltpu.VMEM((2, pairs, wide + hd, wide), BF16),
            pltpu.VMEM((pairs, wide + hd, wide), BF16),
            pltpu.VMEM((nh, own, depth), BF16),
            dma((5,)),
            dma((3,)),
            dma((nh,)),
            dma((nh,)),
            dma((nh,)),
            dma((1,)),
            dma((groups,)),
            dma((groups,)),
            dma((groups, 2)),
            dma((2, groups)),
            dma((chunks, nh)),
            dma((chunks, nh)),
        ],
        compiler_params=pltpu.CompilerParams(
            collective_id=0, has_side_effects=True, vmem_limit_bytes=60 * 2 ** 20),
    )(tokens, w_qkv, lr_weight, lr_base, conv_weight, w_init, w_out)
    total = shares[0].astype(F32)
    for p in range(1, nh):
        total = total + shares[p].astype(F32)
    return total.astype(BF16)


def solution(mesh):
    placed = (
        P(("seq", "head"), None),
        P(None, "head", None),
        P("head", None),
        P("head"),
        P(None, None, "head"),
        P(None, "head", None, None),
        P("head", None),
    )
    return jax.shard_map(
        functools.partial(shards, mesh.shape["seq"], mesh.shape["head"]),
        mesh=mesh, in_specs=placed, out_specs=P(("seq", "head"), None), check_vma=False
    )
```

```python
import functools

import jax
import jax.numpy as jnp
from jax import lax
from jax.experimental import pallas as pl
from jax.experimental.pallas import tpu as pltpu
from jax.sharding import PartitionSpec as P

MB = 16
KERNEL = 4
EPSILON = 1e-05
LANES = 128
MESH = pl.DeviceIdType.MESH
F32, BF16 = jnp.float32, jnp.bfloat16


def mm(a, b):
    return jnp.dot(a, b, preferred_element_type=F32)


def mm_rows(a, b):
    return lax.dot_general(a, b, (((1,), (1,)), ((), ())), preferred_element_type=F32)


def layer(cfg, tok, wqkv, lrw, lrb, cw, winit, wout, shares,
          xbuf, rim, halo, xs, xt, wv, wov, lrwv, cwv, cwt, taps_ref, proj, wi, gate,
          maps, adds, states, sending, reach, kept, given, taken, pbuf,
          lsem, wsem, tsend, trecv, hsend, hrecv, gsend, grecv, rsend, rrecv, psend, precv):
    n, nh, heads, hd, pair_group, chunks = cfg
    own, depth = tok.shape
    rows = own * nh
    inner = heads * hd
    pairs = (heads + 1) // 2
    groups = pairs // pair_group
    wide = 2 * hd
    g, me = lax.axis_index("seq"), lax.axis_index("head")
    not_first, not_last = g > 0, g < n - 1
    core, chip, chips = lax.rem(g, 2), g // 2, n // 2
    other = g + 1 - 2 * core
    chip_before, chip_after = chip > 0, chip < chips - 1
    last_head = me == nh - 1

    small = [pltpu.make_async_copy(a, b, lsem.at[k]) for k, (a, b) in enumerate((
        (tok, xbuf.at[me]), (lrw, lrwv), (cw, cwv), (winit, wi)))]
    for copy in small:
        copy.start()
    weights = []
    thirds = KERNEL - 1
    piece = depth // thirds
    for k in range(thirds):
        cols = pl.ds(k * piece, piece)
        weights.append([pltpu.make_async_copy(
            wqkv.at[c, :, cols], wv.at[c, pl.ds(0, inner), cols], wsem.at[k, c]) for c in range(3)])
        for copy in weights[k]:
            copy.start()
    out_weight = pltpu.make_async_copy(wout, wov, lsem.at[4])

    barrier = pltpu.get_barrier_semaphore()
    for i in range(1, nh):
        pl.semaphore_signal(barrier, inc=1, device_id=(g, lax.rem(me + i, nh)), device_id_type=MESH)

    @pl.when(not_first)
    def _():
        pl.semaphore_signal(barrier, inc=1, device_id=(g - 1, nh - 1), device_id_type=MESH)

    pl.semaphore_signal(barrier, inc=1, device_id=(other, me), device_id_type=MESH)

    @pl.when(chip_before & (core == 1))
    def _():
        pl.semaphore_signal(barrier, inc=1, device_id=(2 * chip - 2 + core, me), device_id_type=MESH)

    @pl.when(chip_after & (core == 0))
    def _():
        pl.semaphore_signal(barrier, inc=1, device_id=(2 * chip + 2 + core, me), device_id_type=MESH)

    relays_on = jnp.where(core == 1, chip_after, chip_before)
    pl.semaphore_wait(barrier, nh + jnp.where(relays_on, 1, 0)
                      + jnp.where(last_head & not_last, nh, 0))

    def token_copy(k, i, slot):
        cols = pl.ds(k * piece, piece)
        return pltpu.make_async_remote_copy(
            src_ref=tok.at[:, cols], dst_ref=xbuf.at[slot, :, cols],
            send_sem=tsend.at[k, i], recv_sem=trecv.at[k, i],
            device_id=(g, lax.rem(me + i, nh)), device_id_type=MESH)

    def halo_copy(h):
        return pltpu.make_async_remote_copy(
            src_ref=rim, dst_ref=halo, send_sem=hsend.at[h], recv_sem=hrecv.at[0],
            device_id=(g + 1, h), device_id_type=MESH)

    for i in range(1, nh):
        token_copy(0, i, me).start()

    small[0].wait()
    rim_rows = KERNEL - 1
    mine_last = xbuf[me].astype(F32)[own - rim_rows:]
    rim[...] = jnp.concatenate(
        [mine_last[r:r + 1, c * piece:(c + 1) * piece] for r in range(rim_rows) for c in range(rim_rows)]
        + [jnp.zeros((rim.shape[0] - rim_rows * rim_rows, piece), F32)], axis=0).astype(BF16)

    @pl.when(last_head & not_last)
    def _():
        for h in range(nh):
            halo_copy(h).start()

    for k in range(1, thirds):
        for i in range(1, nh):
            token_copy(k, i, me).start()

    @pl.when(jnp.logical_not(not_first))
    def _():
        halo[...] = jnp.zeros_like(halo)

    for copy in small[1:]:
        copy.wait()

    cwt[...] = jnp.zeros_like(cwt)
    for c in range(2):
        cwt[pl.ds(c * KERNEL, KERNEL), pl.ds(0, inner)] = cwv[c]
    for j in range(pairs):
        turned = cwt[:, pl.ds(j * LANES, LANES)].T
        for p in range(2 * KERNEL):
            taps_ref[p, pl.ds(j * LANES, LANES), :] = jnp.broadcast_to(turned[:, p:p + 1], (LANES, LANES))

    for way, outer in ((0, jnp.logical_not(chip_before)), (1, jnp.logical_not(chip_after))):
        @pl.when(outer)
        def _():
            for p in range(pairs):
                second = wi[way, 2 * p + 1] if 2 * p + 1 < heads else jnp.zeros((hd, hd), F32)
                states[way, p] = jnp.concatenate([wi[way, 2 * p], second], axis=1).astype(BF16)

    @pl.when(not_first)
    def _():
        halo_copy(0).wait_recv()

    tail = halo[...].astype(F32)
    logit = jnp.zeros((heads, LANES), F32)
    for k in range(thirds):
        cols = pl.ds(k * piece, piece)
        for i in range(1, nh):
            token_copy(k, i, lax.rem(me + nh - i, nh)).wait_recv()
        if own % 16 == 0:
            for p in range(nh):
                xt[pl.ds(p * own, own), cols] = xbuf[p, :, cols]
        else:
            for p in range(nh):
                xs[pl.ds(p * own, own), cols] = xbuf[p, :, cols].astype(F32)
            xt[pl.ds(0, rows), cols] = xs[pl.ds(0, rows), cols].astype(BF16)
        xt[pl.ds(rows, LANES - 16 - rows), cols] = jnp.zeros((LANES - 16 - rows, piece), BF16)
        xt[pl.ds(LANES - 16, 16), cols] = jnp.concatenate(
            [jnp.zeros((16 - rim_rows, piece), F32)]
            + [tail[r * rim_rows + k:r * rim_rows + k + 1] for r in range(rim_rows)], axis=0).astype(BF16)
        for c in range(3):
            weights[k][c].wait()
            share = mm_rows(wv[c, :, cols], xt[:, cols])
            proj[c] = share if k == 0 else proj[c] + share
        logit = logit + mm_rows(lrwv[:, cols], xt[:, cols])

    gate[...] = jax.nn.sigmoid(logit)

    at_s = lax.broadcasted_iota(jnp.int32, (wide, wide), 0)
    at_t = lax.broadcasted_iota(jnp.int32, (wide, wide), 1)
    upper, left_half = at_s < hd, at_t < rows
    same = upper == left_half
    earlier = same & ((at_s // MB) < (at_t // MB))
    causal, anti = same & (at_s <= at_t), same & (at_s >= at_t)
    eye = (at_s == at_t).astype(F32)
    row_left = left_half[:1]

    def diagonal(a):
        return jnp.where(same, jnp.where(upper, a, pltpu.roll(a, rows, 1)), 0.0)

    def root_rate(p):
        first = gate[pl.ds(2 * p, 1), :] * lrb[2 * p]
        if 2 * p + 1 == heads:
            return jnp.sqrt(jnp.where(row_left, first, 0.0) / MB)
        second = gate[pl.ds(2 * p + 1, 1), :] * lrb[2 * p + 1]
        return jnp.sqrt(jnp.where(row_left, first, pltpu.roll(second, rows, 1)) / MB)

    def convolved(c):
        rounded = proj[c].astype(BF16).astype(F32)
        if inner < pairs * wide:
            row = lax.broadcasted_iota(jnp.int32, rounded.shape, 0)
            rounded = jnp.where(row < inner, rounded, 0.0)
        if c == 2:
            return rounded
        total = taps_ref[c * KERNEL + KERNEL - 1] * rounded
        for p in range(KERNEL - 1):
            at = c * KERNEL + p
            total = total + taps_ref[at] * pltpu.roll(rounded, KERNEL - 1 - p, 1)
        return total

    q_all, k_all, v_all = [convolved(c) for c in range(3)]
    out_weight.start()
    each = range(pairs)
    part = [slice(j * wide, (j + 1) * wide) for j in each]
    root = [root_rate(j) for j in each]
    q = [diagonal(q_all[s]) for s in part]
    k = [diagonal(k_all[s]) for s in part]
    k = [k[j] * (root[j] * lax.rsqrt(jnp.sum(k[j] * k[j], axis=0, keepdims=True)
                                     + EPSILON * hd)) for j in each]
    v = [(diagonal(v_all[part[j]]) * root[j]).astype(BF16) for j in each]
    kt = [a.T.astype(BF16) for a in k]
    kb = [a.astype(BF16) for a in k]
    qb = [a.astype(BF16) for a in q]
    gram = [mm(kt[j], jnp.concatenate([kb[j], qb[j]], axis=1)) for j in each]
    one = [jnp.where(earlier, a[:, :wide], 0.0) for a in gram]
    oneb = [a.astype(BF16) for a in one]
    two = [mm(a, a) for a in oneb]
    three = [mm(oneb[j], two[j].astype(BF16)) for j in each]
    inv = [eye - one[j] + two[j] - three[j] for j in each]
    both = [jnp.concatenate([a, a.T], axis=1).astype(BF16) for a in inv]
    kv = [mm(jnp.concatenate([kb[j], v[j]], axis=0), both[j]) for j in each]
    for way, mask in ((0, causal), (1, anti)):
        lhs = [a[:, way * wide:(way + 1) * wide].astype(BF16) for a in kv]
        rhs = [jnp.concatenate(
            [kt[j], jnp.where(mask, gram[j][:, wide:], 0.0).astype(BF16)], axis=1) for j in each]
        made = [mm(lhs[j], rhs[j]) for j in each]
        for j in each:
            p = j
            step = (-made[j][:wide, :wide]).astype(BF16)
            maps[way, p, :, pl.ds(0, wide)] = step
            given[way, p, pl.ds(0, wide), :] = step
            maps[way, p, :, pl.ds(wide, wide)] = (q[j] - made[j][:wide, wide:]).astype(BF16)
            shift = made[j][wide:wide + hd] + made[j][wide + hd:]
            adds[way, p] = shift
            given[way, p, pl.ds(wide, hd), :] = shift[:, :wide].astype(BF16)

    def map_copy(gi):
        span = pl.ds(gi * pair_group, pair_group)
        return pltpu.make_async_remote_copy(
            src_ref=given.at[core, span], dst_ref=taken.at[span],
            send_sem=gsend.at[gi], recv_sem=grecv.at[gi],
            device_id=(other, me), device_id_type=MESH)

    for gi in range(groups):
        map_copy(gi).start()
    relay = 1 - core
    for gi in range(groups):
        map_copy(gi).wait_recv()
        mine = range(gi * pair_group, (gi + 1) * pair_group)
        first = [taken[p] for p in mine]
        then = [mm(a, maps[relay, p]) for a, p in zip(first, mine)]
        for a, b, p in zip(first, then, mine):
            a = a.astype(F32)
            near, far = pl.ds(0, wide), pl.ds(wide, wide)
            maps[relay, p, :, near] = (maps[relay, p, :, near].astype(F32) + a[:wide]
                                       + b[:wide, :wide]).astype(BF16)
            maps[relay, p, :, far] = (maps[relay, p, :, far].astype(F32)
                                      + b[:wide, wide:]).astype(BF16)
            adds[relay, p, :, near] = adds[relay, p, :, near] + a[wide:] + b[wide:, :wide]
            adds[relay, p, :, far] = adds[relay, p, :, far] + b[wide:, wide:]

    def state_copy(way, gi):
        span = pl.ds(gi * pair_group, pair_group)
        return pltpu.make_async_remote_copy(
            src_ref=sending.at[span], dst_ref=states.at[way, span],
            send_sem=rsend.at[gi, 0], recv_sem=rrecv.at[way, gi],
            device_id=(g + 2 * (1 - 2 * way), me), device_id_type=MESH)

    def leaf_copy(way, gi):
        span = pl.ds(gi * pair_group, pair_group)
        return pltpu.make_async_remote_copy(
            src_ref=states.at[way, span], dst_ref=states.at[way, span],
            send_sem=rsend.at[gi, 1], recv_sem=rrecv.at[way, gi],
            device_id=(other, me), device_id_type=MESH)

    normed = []
    for d in range(2):
        way = jnp.where(g < n // 2, d, 1 - d)
        starts = jnp.where(way == 0, chip, chips - 1 - chip) == 0
        onward = (way == relay) & relays_on
        for gi in range(groups):
            @pl.when(jnp.logical_not(starts))
            def _():
                state_copy(way, gi).wait_recv()

            mine = range(gi * pair_group, (gi + 1) * pair_group)
            old = [states[way, p] for p in mine]
            new = [mm(a, maps[way, p]) + adds[way, p] for a, p in zip(old, mine)]

            @pl.when(onward)
            def _():
                for a, b, p in zip(old, new, mine):
                    sending[p] = (a.astype(F32) + b[:, :wide]).astype(BF16)
                state_copy(way, gi).start()

            @pl.when((way == relay) & jnp.logical_not(starts))
            def _():
                leaf_copy(way, gi).start()

            for b, p in zip(new, mine):
                reach[p] = b[:, wide:]

        for p in range(pairs):
            got = reach[p]
            centred = got - jnp.mean(got, axis=0, keepdims=True)
            spread = jnp.mean(centred * centred, axis=0, keepdims=True)
            scaled = centred * lax.rsqrt(spread + EPSILON)
            if d == 0:
                kept[p] = scaled
            else:
                normed.append(scaled + kept[p])

    turned = [a.T for a in normed]
    hidden = jnp.concatenate(
        [jnp.concatenate([a[:rows], a[rows:]], axis=1) for a in turned], axis=1)
    hidden = hidden[:, :inner].astype(BF16)
    out_weight.wait()

    def share_copy(j, i, to, slot):
        cols = pl.ds(j * (depth // chunks), depth // chunks)
        return pltpu.make_async_remote_copy(
            src_ref=pbuf.at[to, :, cols], dst_ref=shares.at[slot, :, cols],
            send_sem=psend.at[j, i], recv_sem=precv.at[j, i],
            device_id=(g, to), device_id_type=MESH)

    for j in range(chunks):
        cols = pl.ds(j * (depth // chunks), depth // chunks)
        share = mm(hidden, wov[:, cols])
        for p in range(nh):
            pbuf[p, :, cols] = share[p * own:(p + 1) * own].astype(BF16)
        for i in range(1, nh):
            share_copy(j, i, lax.rem(me + i, nh), me).start()

    kept_share = pltpu.make_async_copy(pbuf.at[me], shares.at[me], lsem.at[0])
    kept_share.start()
    for j in range(chunks):
        for i in range(1, nh):
            share_copy(j, i, lax.rem(me + i, nh), lax.rem(me + nh - i, nh)).wait_recv()
    kept_share.wait()

    for i in range(1, nh):
        for k in range(thirds):
            token_copy(k, i, me).wait_send()
        for j in range(chunks):
            share_copy(j, i, lax.rem(me + i, nh), me).wait_send()

    @pl.when(last_head & not_last)
    def _():
        for h in range(nh):
            halo_copy(h).wait_send()

    for gi in range(groups):
        map_copy(gi).wait_send()

    @pl.when(relays_on)
    def _():
        for gi in range(groups):
            state_copy(relay, gi).wait_send()

    @pl.when(jnp.where(core == 1, chip_before, chip_after))
    def _():
        for gi in range(groups):
            leaf_copy(relay, gi).wait_send()


def shards(n, nh, tokens, w_qkv, lr_weight, lr_base, conv_weight, w_init, w_out):
    own, depth = tokens.shape
    heads, hd = w_init.shape[1], w_init.shape[2]
    inner = heads * hd
    rows = own * nh
    pairs = (heads + 1) // 2
    padded = pairs * 2 * hd
    pair_group = 2 if pairs % 2 == 0 else 1
    groups = pairs // pair_group
    chunks = 2
    wide = 2 * hd
    hbm = pl.BlockSpec(memory_space=pltpu.HBM)
    smem = pl.BlockSpec(memory_space=pltpu.SMEM)
    dma = pltpu.SemaphoreType.DMA
    shares = pl.pallas_call(
        functools.partial(layer, (n, nh, heads, hd, pair_group, chunks)),
        out_shape=jax.ShapeDtypeStruct((nh, own, depth), BF16),
        in_specs=[hbm, hbm, hbm, smem, hbm, hbm, hbm],
        out_specs=hbm,
        scratch_shapes=[
            pltpu.VMEM((nh, own, depth), BF16),
            pltpu.VMEM((16, depth // (KERNEL - 1)), BF16),
            pltpu.VMEM((16, depth // (KERNEL - 1)), BF16),
            pltpu.VMEM((rows, depth) if own % 16 else (8, LANES), F32),
            pltpu.VMEM((LANES, depth), BF16),
            pltpu.VMEM((3, padded, depth), BF16),
            pltpu.VMEM(w_out.shape, BF16),
            pltpu.VMEM(lr_weight.shape, BF16),
            pltpu.VMEM(conv_weight.shape, F32),
            pltpu.VMEM((LANES, padded), F32),
            pltpu.VMEM((2 * KERNEL, padded, LANES), F32),
            pltpu.VMEM((3, padded, LANES), F32),
            pltpu.VMEM(w_init.shape, F32),
            pltpu.VMEM((heads, LANES), F32),
            pltpu.VMEM((2, pairs, wide, 2 * wide), BF16),
            pltpu.VMEM((2, pairs, hd, 2 * wide), F32),
            pltpu.VMEM((2, pairs, hd, wide), BF16),
            pltpu.VMEM((pairs, hd, wide), BF16),
            pltpu.VMEM((pairs, hd, wide), F32),
            pltpu.VMEM((pairs, hd, wide), F32),
            pltpu.VMEM((2, pairs, wide + hd, wide), BF16),
            pltpu.VMEM((pairs, wide + hd, wide), BF16),
            pltpu.VMEM((nh, own, depth), BF16),
            dma((5,)),
            dma((KERNEL - 1, 3)),
            dma((KERNEL - 1, nh)),
            dma((KERNEL - 1, nh)),
            dma((nh,)),
            dma((1,)),
            dma((groups,)),
            dma((groups,)),
            dma((groups, 2)),
            dma((2, groups)),
            dma((chunks, nh)),
            dma((chunks, nh)),
        ],
        compiler_params=pltpu.CompilerParams(
            collective_id=0, has_side_effects=True, vmem_limit_bytes=60 * 2 ** 20),
    )(tokens, w_qkv, lr_weight, lr_base, conv_weight, w_init, w_out)
    total = shares[0].astype(F32)
    for p in range(1, nh):
        total = total + shares[p].astype(F32)
    return total.astype(BF16)


def solution(mesh):
    placed = (
        P(("seq", "head"), None),
        P(None, "head", None),
        P("head", None),
        P("head"),
        P(None, None, "head"),
        P(None, "head", None, None),
        P("head", None),
    )
    return jax.shard_map(
        functools.partial(shards, mesh.shape["seq"], mesh.shape["head"]),
        mesh=mesh, in_specs=placed, out_specs=P(("seq", "head"), None), check_vma=False
    )
```

```python
import functools

import jax
import jax.numpy as jnp
from jax import lax
from jax.experimental import pallas as pl
from jax.experimental.pallas import tpu as pltpu
from jax.sharding import PartitionSpec as P

MB = 16
KERNEL = 4
EPSILON = 1e-05
LANES = 128
MESH = pl.DeviceIdType.MESH
F32, BF16 = jnp.float32, jnp.bfloat16


def mm(a, b):
    return jnp.dot(a, b, preferred_element_type=F32)


def mm_rows(a, b):
    return lax.dot_general(a, b, (((1,), (1,)), ((), ())), preferred_element_type=F32)


def layer(cfg, tok, wqkv, lrw, lrb, cw, winit, wout, shares,
          xbuf, rim, halo, xs, xt, wv, wov, lrwv, cwv, cwt, taps_ref, proj, wi, gate,
          maps, adds, states, sending, reach, kept, given, taken, pbuf,
          lsem, wsem, tsend, trecv, hsend, hrecv, gsend, grecv, rsend, rrecv, psend, precv):
    n, nh, heads, hd, pair_group, chunks = cfg
    own, depth = tok.shape
    rows = own * nh
    inner = heads * hd
    pairs = (heads + 1) // 2
    groups = pairs // pair_group
    wide = 2 * hd
    g, me = lax.axis_index("seq"), lax.axis_index("head")
    not_first, not_last = g > 0, g < n - 1
    core, chip, chips = lax.rem(g, 2), g // 2, n // 2
    other = g + 1 - 2 * core
    chip_before, chip_after = chip > 0, chip < chips - 1
    last_head = me == nh - 1

    small = [pltpu.make_async_copy(a, b, lsem.at[k]) for k, (a, b) in enumerate((
        (tok, xbuf.at[me]), (lrw, lrwv), (cw, cwv), (winit, wi)))]
    for copy in small:
        copy.start()
    weights = []
    thirds = KERNEL - 1
    piece = depth // thirds
    for k in range(thirds):
        cols = pl.ds(k * piece, piece)
        weights.append([pltpu.make_async_copy(
            wqkv.at[c, :, cols], wv.at[c, pl.ds(0, inner), cols], wsem.at[k, c]) for c in range(3)])
        for copy in weights[k]:
            copy.start()
    out_weight = pltpu.make_async_copy(wout, wov, lsem.at[4])

    barrier = pltpu.get_barrier_semaphore()
    for i in range(1, nh):
        pl.semaphore_signal(barrier, inc=1, device_id=(g, lax.rem(me + i, nh)), device_id_type=MESH)

    @pl.when(not_first)
    def _():
        pl.semaphore_signal(barrier, inc=1, device_id=(g - 1, nh - 1), device_id_type=MESH)

    pl.semaphore_signal(barrier, inc=1, device_id=(other, me), device_id_type=MESH)

    @pl.when(chip_before & (core == 1))
    def _():
        pl.semaphore_signal(barrier, inc=1, device_id=(2 * chip - 2 + core, me), device_id_type=MESH)

    @pl.when(chip_after & (core == 0))
    def _():
        pl.semaphore_signal(barrier, inc=1, device_id=(2 * chip + 2 + core, me), device_id_type=MESH)

    relays_on = jnp.where(core == 1, chip_after, chip_before)
    pl.semaphore_wait(barrier, nh + jnp.where(relays_on, 1, 0)
                      + jnp.where(last_head & not_last, nh, 0))

    def token_copy(k, i, slot):
        cols = pl.ds(k * piece, piece)
        return pltpu.make_async_remote_copy(
            src_ref=tok.at[:, cols], dst_ref=xbuf.at[slot, :, cols],
            send_sem=tsend.at[k, i], recv_sem=trecv.at[k, i],
            device_id=(g, lax.rem(me + i, nh)), device_id_type=MESH)

    def halo_copy(h):
        return pltpu.make_async_remote_copy(
            src_ref=rim, dst_ref=halo, send_sem=hsend.at[h], recv_sem=hrecv.at[0],
            device_id=(g + 1, h), device_id_type=MESH)

    for i in range(1, nh):
        token_copy(0, i, me).start()

    small[0].wait()
    rim_rows = KERNEL - 1
    mine_last = xbuf[me].astype(F32)[own - rim_rows:]
    rim[...] = jnp.concatenate(
        [mine_last[r:r + 1, c * piece:(c + 1) * piece] for r in range(rim_rows) for c in range(rim_rows)]
        + [jnp.zeros((rim.shape[0] - rim_rows * rim_rows, piece), F32)], axis=0).astype(BF16)

    @pl.when(last_head & not_last)
    def _():
        for h in range(nh):
            halo_copy(h).start()

    for k in range(1, thirds):
        for i in range(1, nh):
            token_copy(k, i, me).start()

    @pl.when(jnp.logical_not(not_first))
    def _():
        halo[...] = jnp.zeros_like(halo)

    for copy in small[1:]:
        copy.wait()

    cwt[...] = jnp.zeros_like(cwt)
    for c in range(2):
        cwt[pl.ds(c * KERNEL, KERNEL), pl.ds(0, inner)] = cwv[c]
    for j in range(pairs):
        turned = cwt[:, pl.ds(j * LANES, LANES)].T
        for p in range(2 * KERNEL):
            taps_ref[p, pl.ds(j * LANES, LANES), :] = jnp.broadcast_to(turned[:, p:p + 1], (LANES, LANES))

    for way, outer in ((0, jnp.logical_not(chip_before)), (1, jnp.logical_not(chip_after))):
        @pl.when(outer)
        def _():
            for p in range(pairs):
                second = wi[way, 2 * p + 1] if 2 * p + 1 < heads else jnp.zeros((hd, hd), F32)
                states[way, p] = jnp.concatenate([wi[way, 2 * p], second], axis=1).astype(BF16)

    @pl.when(not_first)
    def _():
        halo_copy(0).wait_recv()

    tail = halo[...].astype(F32)
    logit = jnp.zeros((heads, LANES), F32)
    for k in range(thirds):
        cols = pl.ds(k * piece, piece)
        for i in range(1, nh):
            token_copy(k, i, lax.rem(me + nh - i, nh)).wait_recv()
        if own % 16 == 0:
            for p in range(nh):
                xt[pl.ds(p * own, own), cols] = xbuf[p, :, cols]
        else:
            for p in range(nh):
                xs[pl.ds(p * own, own), cols] = xbuf[p, :, cols].astype(F32)
            xt[pl.ds(0, rows), cols] = xs[pl.ds(0, rows), cols].astype(BF16)
        xt[pl.ds(rows, LANES - 16 - rows), cols] = jnp.zeros((LANES - 16 - rows, piece), BF16)
        xt[pl.ds(LANES - 16, 16), cols] = jnp.concatenate(
            [jnp.zeros((16 - rim_rows, piece), F32)]
            + [tail[r * rim_rows + k:r * rim_rows + k + 1] for r in range(rim_rows)], axis=0).astype(BF16)
        for c in range(3):
            weights[k][c].wait()
            share = mm_rows(wv[c, :, cols], xt[:, cols])
            proj[c] = share if k == 0 else proj[c] + share
        logit = logit + mm_rows(lrwv[:, cols], xt[:, cols])

    gate[...] = jax.nn.sigmoid(logit)

    at_s = lax.broadcasted_iota(jnp.int32, (wide, wide), 0)
    at_t = lax.broadcasted_iota(jnp.int32, (wide, wide), 1)
    upper, left_half = at_s < hd, at_t < rows
    same = upper == left_half
    earlier = same & ((at_s // MB) < (at_t // MB))
    causal, anti = same & (at_s <= at_t), same & (at_s >= at_t)
    eye = (at_s == at_t).astype(F32)
    row_left = left_half[:1]

    def diagonal(a):
        return jnp.where(same, jnp.where(upper, a, pltpu.roll(a, rows, 1)), 0.0)

    def root_rate(p):
        first = gate[pl.ds(2 * p, 1), :] * lrb[2 * p]
        if 2 * p + 1 == heads:
            return jnp.sqrt(jnp.where(row_left, first, 0.0) / MB)
        second = gate[pl.ds(2 * p + 1, 1), :] * lrb[2 * p + 1]
        return jnp.sqrt(jnp.where(row_left, first, pltpu.roll(second, rows, 1)) / MB)

    def convolved(c):
        rounded = proj[c].astype(BF16).astype(F32)
        if inner < pairs * wide:
            row = lax.broadcasted_iota(jnp.int32, rounded.shape, 0)
            rounded = jnp.where(row < inner, rounded, 0.0)
        if c == 2:
            return rounded
        total = taps_ref[c * KERNEL + KERNEL - 1] * rounded
        for p in range(KERNEL - 1):
            at = c * KERNEL + p
            total = total + taps_ref[at] * pltpu.roll(rounded, KERNEL - 1 - p, 1)
        return total

    q_all, k_all, v_all = [convolved(c) for c in range(3)]
    out_weight.start()
    each = range(pairs)
    part = [slice(j * wide, (j + 1) * wide) for j in each]
    root = [root_rate(j) for j in each]
    q = [diagonal(q_all[s]) for s in part]
    k = [diagonal(k_all[s]) for s in part]
    k = [k[j] * (root[j] * lax.rsqrt(jnp.sum(k[j] * k[j], axis=0, keepdims=True)
                                     + EPSILON * hd)) for j in each]
    v = [(diagonal(v_all[part[j]]) * root[j]).astype(BF16) for j in each]
    kt = [a.T.astype(BF16) for a in k]
    kb = [a.astype(BF16) for a in k]
    qb = [a.astype(BF16) for a in q]
    gram = [mm(kt[j], jnp.concatenate([kb[j], qb[j]], axis=1)) for j in each]
    one = [jnp.where(earlier, a[:, :wide], 0.0) for a in gram]
    oneb = [a.astype(BF16) for a in one]
    two = [mm(a, a) for a in oneb]
    three = [mm(oneb[j], two[j].astype(BF16)) for j in each]
    inv = [eye - one[j] + two[j] - three[j] for j in each]
    both = [jnp.concatenate([a, a.T], axis=1).astype(BF16) for a in inv]
    kv = [mm(jnp.concatenate([kb[j], v[j]], axis=0), both[j]) for j in each]
    lhs = [[a[:, way * wide:(way + 1) * wide].astype(BF16) for a in kv] for way in range(2)]

    def map_copy(gi):
        span = pl.ds(gi * pair_group, pair_group)
        return pltpu.make_async_remote_copy(
            src_ref=given.at[core, span], dst_ref=taken.at[span],
            send_sem=gsend.at[gi], recv_sem=grecv.at[gi],
            device_id=(other, me), device_id_type=MESH)

    near, far = pl.ds(0, wide), pl.ds(wide, wide)
    for gi in range(groups):
        for way in range(2):
            for p in range(gi * pair_group, (gi + 1) * pair_group):
                made = mm(lhs[way][p], kt[p])
                step = (-made[:wide]).astype(BF16)
                shift = made[wide:wide + hd] + made[wide + hd:]
                maps[way, p, :, near] = step
                adds[way, p, :, near] = shift
                given[way, p, near, :] = step
                given[way, p, pl.ds(wide, hd), :] = shift.astype(BF16)
        map_copy(gi).start()

    for way, mask in ((0, causal), (1, anti)):
        for p in each:
            score = jnp.where(mask, gram[p][:, wide:], 0.0).astype(BF16)
            made = mm(lhs[way][p], score)
            maps[way, p, :, far] = (q[p] - made[:wide]).astype(BF16)
            adds[way, p, :, far] = made[wide:wide + hd] + made[wide + hd:]

    relay = 1 - core
    for gi in range(groups):
        map_copy(gi).wait_recv()
        mine = range(gi * pair_group, (gi + 1) * pair_group)
        first = [taken[p] for p in mine]
        then = [mm(a, maps[relay, p]) for a, p in zip(first, mine)]
        for a, b, p in zip(first, then, mine):
            a = a.astype(F32)
            maps[relay, p, :, near] = (maps[relay, p, :, near].astype(F32) + a[:wide]
                                       + b[:wide, :wide]).astype(BF16)
            maps[relay, p, :, far] = (maps[relay, p, :, far].astype(F32)
                                      + b[:wide, wide:]).astype(BF16)
            adds[relay, p, :, near] = adds[relay, p, :, near] + a[wide:] + b[wide:, :wide]
            adds[relay, p, :, far] = adds[relay, p, :, far] + b[wide:, wide:]

    def state_copy(way, gi):
        span = pl.ds(gi * pair_group, pair_group)
        return pltpu.make_async_remote_copy(
            src_ref=sending.at[span], dst_ref=states.at[way, span],
            send_sem=rsend.at[gi, 0], recv_sem=rrecv.at[way, gi],
            device_id=(g + 2 * (1 - 2 * way), me), device_id_type=MESH)

    def leaf_copy(way, gi):
        span = pl.ds(gi * pair_group, pair_group)
        return pltpu.make_async_remote_copy(
            src_ref=states.at[way, span], dst_ref=states.at[way, span],
            send_sem=rsend.at[gi, 1], recv_sem=rrecv.at[way, gi],
            device_id=(other, me), device_id_type=MESH)

    normed = []
    for d in range(2):
        way = jnp.where(g < n // 2, d, 1 - d)
        starts = jnp.where(way == 0, chip, chips - 1 - chip) == 0
        onward = (way == relay) & relays_on
        for gi in range(groups):
            @pl.when(jnp.logical_not(starts))
            def _():
                state_copy(way, gi).wait_recv()

            @pl.when((way == relay) & jnp.logical_not(starts))
            def _():
                leaf_copy(way, gi).start()

            mine = range(gi * pair_group, (gi + 1) * pair_group)
            old = [states[way, p] for p in mine]
            new = [mm(a, maps[way, p]) + adds[way, p] for a, p in zip(old, mine)]

            @pl.when(onward)
            def _():
                for a, b, p in zip(old, new, mine):
                    sending[p] = (a.astype(F32) + b[:, :wide]).astype(BF16)
                state_copy(way, gi).start()

            for b, p in zip(new, mine):
                reach[p] = b[:, wide:]

        for p in range(pairs):
            got = reach[p]
            centred = got - jnp.mean(got, axis=0, keepdims=True)
            spread = jnp.mean(centred * centred, axis=0, keepdims=True)
            scaled = centred * lax.rsqrt(spread + EPSILON)
            if d == 0:
                kept[p] = scaled
            else:
                normed.append(scaled + kept[p])

    turned = [a.T for a in normed]
    hidden = jnp.concatenate(
        [jnp.concatenate([a[:rows], a[rows:]], axis=1) for a in turned], axis=1)
    hidden = hidden[:, :inner].astype(BF16)
    out_weight.wait()

    def share_copy(j, i, to, slot):
        cols = pl.ds(j * (depth // chunks), depth // chunks)
        return pltpu.make_async_remote_copy(
            src_ref=pbuf.at[to, :, cols], dst_ref=shares.at[slot, :, cols],
            send_sem=psend.at[j, i], recv_sem=precv.at[j, i],
            device_id=(g, to), device_id_type=MESH)

    for j in range(chunks):
        cols = pl.ds(j * (depth // chunks), depth // chunks)
        share = mm(hidden, wov[:, cols])
        for p in range(nh):
            pbuf[p, :, cols] = share[p * own:(p + 1) * own].astype(BF16)
        for i in range(1, nh):
            share_copy(j, i, lax.rem(me + i, nh), me).start()

    kept_share = pltpu.make_async_copy(pbuf.at[me], shares.at[me], lsem.at[0])
    kept_share.start()
    for j in range(chunks):
        for i in range(1, nh):
            share_copy(j, i, lax.rem(me + i, nh), lax.rem(me + nh - i, nh)).wait_recv()
    kept_share.wait()

    for i in range(1, nh):
        for k in range(thirds):
            token_copy(k, i, me).wait_send()
        for j in range(chunks):
            share_copy(j, i, lax.rem(me + i, nh), me).wait_send()

    @pl.when(last_head & not_last)
    def _():
        for h in range(nh):
            halo_copy(h).wait_send()

    for gi in range(groups):
        map_copy(gi).wait_send()

    @pl.when(relays_on)
    def _():
        for gi in range(groups):
            state_copy(relay, gi).wait_send()

    @pl.when(jnp.where(core == 1, chip_before, chip_after))
    def _():
        for gi in range(groups):
            leaf_copy(relay, gi).wait_send()


def shards(n, nh, tokens, w_qkv, lr_weight, lr_base, conv_weight, w_init, w_out):
    own, depth = tokens.shape
    heads, hd = w_init.shape[1], w_init.shape[2]
    inner = heads * hd
    rows = own * nh
    pairs = (heads + 1) // 2
    padded = pairs * 2 * hd
    pair_group = max(k for k in (1, 2, 3) if pairs % k == 0)
    groups = pairs // pair_group
    chunks = 2
    wide = 2 * hd
    hbm = pl.BlockSpec(memory_space=pltpu.HBM)
    smem = pl.BlockSpec(memory_space=pltpu.SMEM)
    dma = pltpu.SemaphoreType.DMA
    shares = pl.pallas_call(
        functools.partial(layer, (n, nh, heads, hd, pair_group, chunks)),
        out_shape=jax.ShapeDtypeStruct((nh, own, depth), BF16),
        in_specs=[hbm, hbm, hbm, smem, hbm, hbm, hbm],
        out_specs=hbm,
        scratch_shapes=[
            pltpu.VMEM((nh, own, depth), BF16),
            pltpu.VMEM((16, depth // (KERNEL - 1)), BF16),
            pltpu.VMEM((16, depth // (KERNEL - 1)), BF16),
            pltpu.VMEM((rows, depth) if own % 16 else (8, LANES), F32),
            pltpu.VMEM((LANES, depth), BF16),
            pltpu.VMEM((3, padded, depth), BF16),
            pltpu.VMEM(w_out.shape, BF16),
            pltpu.VMEM(lr_weight.shape, BF16),
            pltpu.VMEM(conv_weight.shape, F32),
            pltpu.VMEM((LANES, padded), F32),
            pltpu.VMEM((2 * KERNEL, padded, LANES), F32),
            pltpu.VMEM((3, padded, LANES), F32),
            pltpu.VMEM(w_init.shape, F32),
            pltpu.VMEM((heads, LANES), F32),
            pltpu.VMEM((2, pairs, wide, 2 * wide), BF16),
            pltpu.VMEM((2, pairs, hd, 2 * wide), F32),
            pltpu.VMEM((2, pairs, hd, wide), BF16),
            pltpu.VMEM((pairs, hd, wide), BF16),
            pltpu.VMEM((pairs, hd, wide), F32),
            pltpu.VMEM((pairs, hd, wide), F32),
            pltpu.VMEM((2, pairs, wide + hd, wide), BF16),
            pltpu.VMEM((pairs, wide + hd, wide), BF16),
            pltpu.VMEM((nh, own, depth), BF16),
            dma((5,)),
            dma((KERNEL - 1, 3)),
            dma((KERNEL - 1, nh)),
            dma((KERNEL - 1, nh)),
            dma((nh,)),
            dma((1,)),
            dma((groups,)),
            dma((groups,)),
            dma((groups, 2)),
            dma((2, groups)),
            dma((chunks, nh)),
            dma((chunks, nh)),
        ],
        compiler_params=pltpu.CompilerParams(
            collective_id=0, has_side_effects=True, vmem_limit_bytes=60 * 2 ** 20),
    )(tokens, w_qkv, lr_weight, lr_base, conv_weight, w_init, w_out)
    total = shares[0].astype(F32)
    for p in range(1, nh):
        total = total + shares[p].astype(F32)
    return total.astype(BF16)


def solution(mesh):
    placed = (
        P(("seq", "head"), None),
        P(None, "head", None),
        P("head", None),
        P("head"),
        P(None, None, "head"),
        P(None, "head", None, None),
        P("head", None),
    )
    return jax.shard_map(
        functools.partial(shards, mesh.shape["seq"], mesh.shape["head"]),
        mesh=mesh, in_specs=placed, out_specs=P(("seq", "head"), None), check_vma=False
    )
```
